512 devices in a mesh: dp: 8 (over z_hi, core), ctx: 64 (over z_lo, x, y).
Axes of the slice: x: 4, y: 4, z: 16 (z_hi: 4, z_lo: 4; z = z_hi * 4 + z_lo), core: 2. Of those that a mesh axis runs over, the one named last changes fastest.
Arguments:
- inputs: bfloat16 [8, 8192, 4096], P('dp', 'ctx'), may hold values from -0.0234375 to 0.0234375
- grad_out: bfloat16 [8, 8192, 4096], P('dp', 'ctx'), may hold values from -6 to 6
- filt: bfloat16 [8192, 4096], P('ctx'), may hold values from -1.5 to 1.5
Outputs:
- input_grad: bfloat16 [8, 8192, 4096], P('dp', 'ctx')
- filter_grad: float32 [8192, 4096], P('ctx', 'dp')
The draws below stay inside these ranges and needn't reach their ends.
All inputs are finite; a program needn't handle non-finite values.
Results may differ from the reference program's by a relative error of at most 0.005.
Values may be sent and summed in bfloat16 or wider, within the bound.
A program may use at most 128 MiB of HBM per device.

```python
import math
import jax
import jax.numpy as jnp
from jax import lax

CH = 4096
SEQ = 8192
SEGS = 8
N_DP = 8


def draw_filt(key, part):
    key = jax.random.fold_in(key, 7)
    key_decay, key_noise = jax.random.split(key)
    lag = jnp.arange(SEQ, dtype=jnp.float32)[:, None]
    lowest = jnp.log(jnp.float32(30.0))
    noise = jnp.clip(jax.random.normal(key_noise, (SEQ, CH), jnp.float32), -4.0, 4.0)
    highest = jnp.log(jnp.float32(SEQ) * 4.0)
    spread = jax.random.uniform(key_decay, (1, CH), jnp.float32)
    memory = jnp.exp(lowest + (highest - lowest) * spread)
    amplitude = jnp.sqrt((1.0 - jnp.exp(-2.0 / memory)) / (1.0 - jnp.exp(-2.0 * SEQ / memory)))
    return (amplitude * jnp.exp(-lag / memory) * noise).astype(jnp.bfloat16)


def strengthened(values, own_key, source, target, blocks, factor):
    def block_of(dim):
        return (jnp.arange(values.shape[dim]) // (values.shape[dim] // blocks)).reshape((-1,) + (1,) * (values.ndim - 1 - dim))

    one_side = jax.random.permutation(own_key, blocks)[block_of(target)]
    second = (block_of(target) + blocks // 2) % blocks
    return jnp.where((block_of(source) == one_side) | (block_of(source) == second), factor * values, values)


def level_of(own_key, extent, cuts, smallest, high):
    def one(axis_at, shards_of):
        steps = jax.random.uniform(jax.random.fold_in(jax.random.fold_in(own_key, 6), axis_at), (shards_of,), jnp.float32, smallest / len(cuts), high / len(cuts))
        return jnp.repeat(jnp.exp(steps), extent[axis_at] // shards_of).reshape((-1,) + (1,) * (len(extent) - axis_at - 1))

    factor_of = one(*cuts[0])
    for cut in cuts[1:]:
        factor_of = factor_of * one(*cut)
    return factor_of


def scatter_about(rng, extent, scale, limit, pieces=(), kind=jnp.bfloat16):
    result = jax.random.normal(rng, extent, jnp.float32) * scale
    if len(pieces) > 0:
        result = level_of(rng, extent, pieces, -0.22, 0.18) * result
    return jnp.clip(result, min=-limit, max=limit).astype(kind)


def noise_with(own_key, dims, scale, limit, pieces, heavy, kind=jnp.bfloat16):
    array = scale * jax.random.normal(own_key, dims, jnp.float32)
    if pieces:
        array = array * level_of(own_key, dims, pieces, -0.22, 0.18)
    return jnp.clip(strengthened(array, jax.random.fold_in(own_key, 3), *heavy), -limit, limit).astype(kind)


def setup_inputs(seed: int = 0) -> dict:
    seeds = jax.random.split(jax.random.key(seed), 4)
    inputs = scatter_about(seeds[0], (SEGS, SEQ, CH), (N_DP * SEQ) ** -0.5, 0.0234375, ((0, 8), (1, 64)))
    grad_out = noise_with(seeds[1], (SEGS, SEQ, CH), 1.0, 6.0, ((0, 8), (1, 64)), (0, 2, 8, 2.0))
    filt = draw_filt(jax.random.fold_in(seeds[3], 71), 0)
    return dict(inputs=inputs, grad_out=grad_out, filt=filt)


def reference(inputs, grad_out, filt):
    length = 2 * SEQ
    width = math.gcd(CH, 256)
    groups = CH // width

    def block(index):
        start = index * width
        signal = lax.dynamic_slice_in_dim(inputs, start, width, 2).astype(jnp.float32)
        upstream = lax.dynamic_slice_in_dim(grad_out, start, width, 2).astype(jnp.float32)
        kernel = lax.dynamic_slice_in_dim(filt, start, width, 1).astype(jnp.float32)
        spec_signal = jnp.fft.rfft(signal, n=length, axis=1)
        spec_upstream = jnp.fft.rfft(upstream, n=length, axis=1)
        spec_kernel = jnp.fft.rfft(kernel, n=length, axis=0)
        grad_signal = jnp.fft.irfft(jnp.conj(spec_kernel)[None] * spec_upstream, n=length, axis=1)[:, :SEQ]
        terms = jnp.fft.irfft(jnp.conj(spec_signal) * spec_upstream, n=length, axis=1)[:, :SEQ]
        grad_kernel = jnp.sum(terms.astype(jnp.float32), axis=0)
        return grad_signal.astype(jnp.bfloat16), grad_kernel.astype(jnp.float32)

    grad_signal, grad_kernel = lax.map(block, jnp.arange(groups, dtype=jnp.int32))
    input_grad = grad_signal.transpose(1, 2, 0, 3).reshape(SEGS, SEQ, CH)
    filter_grad = grad_kernel.transpose(1, 0, 2).reshape(SEQ, CH)
    return input_grad, filter_grad
```

```python
import math
import numpy as np
import jax
import jax.numpy as jnp
from jax import lax
from jax.experimental import pallas as pl
from jax.experimental.pallas import tpu as pltpu
from jax.sharding import PartitionSpec as P

N = 16384
KN = 65


def cmul_const(v, c, s):
    re, im = v
    if abs(s) < 1e-12 and abs(c - 1) < 1e-12:
        return v
    if abs(c) < 1e-12 and abs(s - 1) < 1e-12:
        return (-im, re)
    if abs(c) < 1e-12 and abs(s + 1) < 1e-12:
        return (im, -re)
    if abs(abs(c) - abs(s)) < 1e-12:
        h = abs(c)
        sc, ss = (1.0 if c > 0 else -1.0), (1.0 if s > 0 else -1.0)
        a = re * h
        b = im * h
        first = (a if sc > 0 else -a)
        first = first - b if ss > 0 else first + b
        second = (b if sc > 0 else -b)
        second = second + a if ss > 0 else second - a
        return (first, second)
    return (re * c - im * s, re * s + im * c)


def fft_complex(values, sign):
    n = len(values)
    if n == 1:
        return values
    if n == 2:
        (ar, ai), (br, bi) = values
        return [(ar + br, ai + bi), (ar - br, ai - bi)]
    if n % 4 == 0:
        quarter = n // 4
        parts = [fft_complex(values[r::4], sign) for r in range(4)]
        out = [None] * n
        for k in range(quarter):
            turned = []
            for r in range(4):
                angle = sign * 2.0 * math.pi * r * k / n
                turned.append(cmul_const(parts[r][k], math.cos(angle), math.sin(angle)))
            (ar, ai), (br, bi), (cr, ci), (dr, di) = turned
            s0r, s0i, s1r, s1i = ar + cr, ai + ci, ar - cr, ai - ci
            s2r, s2i, s3r, s3i = br + dr, bi + di, br - dr, bi - di
            out[k] = (s0r + s2r, s0i + s2i)
            out[k + 2 * quarter] = (s0r - s2r, s0i - s2i)
            if sign < 0:
                out[k + quarter] = (s1r + s3i, s1i - s3r)
                out[k + 3 * quarter] = (s1r - s3i, s1i + s3r)
            else:
                out[k + quarter] = (s1r - s3i, s1i + s3r)
                out[k + 3 * quarter] = (s1r + s3i, s1i - s3r)
        return out
    half = n // 2
    even = fft_complex(values[0::2], sign)
    odd = fft_complex(values[1::2], sign)
    out = [None] * n
    for k in range(half):
        angle = sign * 2.0 * math.pi * k / n
        tr, ti = cmul_const(odd[k], math.cos(angle), math.sin(angle))
        er, ei = even[k]
        out[k] = (er + tr, ei + ti)
        out[k + half] = (er - tr, ei - ti)
    return out


def odd_bins(values, period):
    quarter = period // 4
    turned = []
    for a in range(quarter):
        angle = -2.0 * math.pi * a / period
        turned.append(cmul_const((values[a], -values[a + quarter]), math.cos(angle), math.sin(angle)))
    spectrum = fft_complex(turned, -1.0)
    found = {}
    for l in range(quarter):
        k = 4 * l + 1
        re, im = spectrum[l]
        if k <= period // 2:
            found[k] = (re, im)
        else:
            found[period - k] = (re, -im)
    return found


def real_bins(values):
    n = len(values)
    if n == 2:
        return {0: (values[0] + values[1], None), 1: (values[0] - values[1], None)}
    half = n // 2
    sums = [values[a] + values[a + half] for a in range(half)]
    diffs = [values[a] - values[a + half] for a in range(half)]
    found = {2 * k: v for k, v in real_bins(sums).items()}
    found.update(odd_bins(diffs, n))
    return found


def padded_bins(values):
    found = odd_bins(values, 2 * len(values))
    found.update({2 * k: v for k, v in real_bins(values).items()})
    return found


def odd_values(bins, period):
    quarter = period // 4
    spectrum = []
    for l in range(quarter):
        k = 4 * l + 1
        if k <= period // 2:
            spectrum.append(bins[k])
        else:
            re, im = bins[period - k]
            spectrum.append((re, -im))
    turned = fft_complex(spectrum, 1.0)
    lower, upper = [], []
    for a in range(quarter):
        angle = 2.0 * math.pi * a / period
        re, im = cmul_const(turned[a], math.cos(angle), math.sin(angle))
        lower.append(re)
        upper.append(-im)
    return lower + upper


def real_values(bins, n):
    if n == 2:
        return [bins[0][0] + bins[1][0], bins[0][0] - bins[1][0]]
    sums = real_values({k // 2: v for k, v in bins.items() if k % 2 == 0}, n // 2)
    diffs = odd_values(bins, n)
    return [s + d for s, d in zip(sums, diffs)] + [s - d for s, d in zip(sums, diffs)]


def padded_values(bins, n):
    odd = odd_values(bins, 2 * n)
    even = real_values({k // 2: v for k, v in bins.items() if k % 2 == 0}, n)
    return [o + e for o, e in zip(odd, even)]


def big_tables():
    m = np.arange(128)
    grid = (m[:, None] * m[None, :] % 128) * (2.0 * np.pi / 128)
    c, s = np.cos(grid), np.sin(grid)
    full = np.block([[c, -s], [s, c]]).astype(np.float32)
    high = full.astype(jnp.bfloat16)
    low = (full - high.astype(np.float32)).astype(jnp.bfloat16)
    turn = np.arange(72)[:, None] * m[None, :] * (2.0 * np.pi / N)
    return high, low, np.cos(turn).astype(np.float32), np.sin(turn).astype(np.float32)


def spectra_of(recv_ref, y_ref, tr_ref, ti_ref, group):
    rows = pl.ds(pl.multiple_of(group * 16, 16), 16)
    values = [recv_ref[a, rows, :].astype(jnp.float32) for a in range(64)]
    bins = padded_bins(values)
    for k in range(KN):
        re, im = bins[k]
        tr, ti = tr_ref[pl.ds(k, 1), :], ti_ref[pl.ds(k, 1), :]
        if im is None:
            re, im = re * tr, -(re * ti)
        else:
            re, im = re * tr + im * ti, im * tr - re * ti
        y_ref[k, rows, pl.ds(0, 128)] = re.astype(jnp.bfloat16)
        y_ref[k, rows, pl.ds(128, 128)] = im.astype(jnp.bfloat16)


def dot_t(x, table):
    return lax.dot_general(x, table, (((1,), (1,)), ((), ())), preferred_element_type=jnp.float32)


def dot_n(x, table):
    return jnp.dot(x, table, preferred_element_type=jnp.float32)


KC = 5


def mix(step, y_ref, hi_ref, lo_ref, v_ref):
    k0 = step * KC
    y = y_ref[pl.ds(k0, KC)].reshape(KC * 160, 256)
    spec = (dot_n(y, hi_ref[...]) + dot_n(y, lo_ref[...])).reshape(KC, 160, 256)
    prods = []
    for i in range(KC):
        k = k0 + i
        ur, ui = spec[i, 0:64, :128], spec[i, 0:64, 128:]
        sr, si = spec[i, 64:128, :128], spec[i, 64:128, 128:]
        kr, ki = spec[i, 128:160, :128], spec[i, 128:160, 128:]
        scale = jnp.where((k == 0) | (k == 64), 1.0 / N, 2.0 / N).astype(jnp.float32)
        ur, ui = ur * scale, ui * scale
        kr = jnp.concatenate([kr, kr], axis=0)
        ki = jnp.concatenate([ki, ki], axis=0)
        pr = kr * ur + ki * ui
        pi = kr * ui - ki * ur
        qr = sr * ur + si * ui
        qi = sr * ui - si * ur
        qr = qr[0:32] + qr[32:64]
        qi = qi[0:32] + qi[32:64]
        re = jnp.concatenate([pr, qr], axis=0)
        im = jnp.concatenate([pi, qi], axis=0)
        prods.append(jnp.concatenate([re, im], axis=1).astype(jnp.bfloat16))
    prod = jnp.concatenate(prods, axis=0)
    back = dot_t(prod, hi_ref[...]) + dot_t(prod, lo_ref[...])
    v_ref[pl.ds(k0, KC)] = back.reshape(KC, 96, 256)


def values_of(v_ref, tr_ref, ti_ref, rows):
    bins = {}
    for k in range(KN):
        re, im = v_ref[k, rows, pl.ds(0, 128)], v_ref[k, rows, pl.ds(128, 128)]
        tr, ti = tr_ref[pl.ds(k, 1), :], ti_ref[pl.ds(k, 1), :]
        if k in (0, 64):
            bins[k] = (re * tr - im * ti, None)
        else:
            bins[k] = (re * tr - im * ti, im * tr + re * ti)
    return padded_values(bins, 64)


def compute_kernel(recv_ref, hi_ref, lo_ref, tr_ref, ti_ref, ig_ref, fg_ref, y_ref, v_ref):
    def first(group, carry):
        spectra_of(recv_ref, y_ref, tr_ref, ti_ref, group)
        return carry

    lax.fori_loop(0, 10, first, 0)

    def second(k, carry):
        mix(k, y_ref, hi_ref, lo_ref, v_ref)
        return carry

    lax.fori_loop(0, KN // KC, second, 0)

    def third(group, carry):
        rows = pl.ds(pl.multiple_of(group * 16, 16), 16)
        out = values_of(v_ref, tr_ref, ti_ref, rows)
        for a in range(64):
            ig_ref[a, group // 2, pl.ds(pl.multiple_of((group % 2) * 16, 16), 16), :] = out[a].astype(jnp.bfloat16)
        return carry

    lax.fori_loop(0, 4, third, 0)

    def fourth(group, carry):
        rows = pl.ds(pl.multiple_of(64 + group * 16, 16), 16)
        out = values_of(v_ref, tr_ref, ti_ref, rows)
        for a in range(0, 64, 2):
            for h in range(2):
                pair = jnp.concatenate([out[a][8 * h:8 * h + 8], out[a + 1][8 * h:8 * h + 8]], axis=0)
                fg_ref[2 * group + h, a // 2, :, :] = pair.astype(jnp.bfloat16)
        return carry

    lax.fori_loop(0, 2, fourth, 0)


def compute_call(recv):
    tables = [jnp.asarray(t) for t in big_tables()]
    return pl.pallas_call(
        compute_kernel,
        out_shape=(
            jax.ShapeDtypeStruct((64, 2, 32, 128), jnp.bfloat16),
            jax.ShapeDtypeStruct((4, 32, 16, 128), jnp.bfloat16),
        ),
        in_specs=[vmem()] * 5,
        out_specs=(vmem(), vmem()),
        scratch_shapes=[
            pltpu.VMEM((KN, 160, 256), jnp.bfloat16),
            pltpu.VMEM((KN, 96, 256), jnp.float32),
        ],
        compiler_params=pltpu.CompilerParams(vmem_limit_bytes=56 * 1024 * 1024),
    )(recv, *tables)


def copy_to(src, dst, send_sem, recv_sem, dp, ctx):
    return pltpu.make_async_remote_copy(
        src_ref=src,
        dst_ref=dst,
        send_sem=send_sem,
        recv_sem=recv_sem,
        device_id=(dp, ctx),
        device_id_type=pl.DeviceIdType.MESH,
    )


def wait_bytes(ref, sem):
    pltpu.make_async_copy(ref, ref, sem).wait()


def partner(me, i):
    return ((me // 16 + i % 4) % 4) * 16 + (me % 16 + i // 4) % 16


def to_pieces(x_ref, st_ref, g, j, index):
    parts = []
    for q in range(4):
        cols = pl.ds(pl.multiple_of(512 * (2 * q + j) + 128 * g, 128), 128)
        parts.append(x_ref[:, cols].astype(jnp.float32).T.reshape(16, 8, 128))
    owners = pl.ds(pl.multiple_of(16 * g, 16), 16)
    index(owners)[...] = jnp.concatenate(parts, axis=1).astype(jnp.bfloat16)


def gather_kernel(up_ref, sig_ref, filt_ref, out_ref, up_st, sig_st, filt_st, send_sem, recv_sem):
    dp = lax.axis_index("dp")
    me = lax.axis_index("ctx")
    core, high = dp % 2, dp // 2

    def send_signal(which, x_ref, st_ref):
        def turn(i, carry):
            g, j = i // 2, i % 2
            to_pieces(x_ref, st_ref, g, j, lambda owners: st_ref.at[owners, j])
            return carry

        lax.fori_loop(0, 8, turn, 0)
        rows = pl.ds(pl.multiple_of(64 * which + 32 * core, 32), 32)
        pltpu.make_async_copy(st_ref.at[me, core], out_ref.at[me, rows], recv_sem.at[which]).start()
        copy_to(
            st_ref.at[me, 1 - core], out_ref.at[me, rows], send_sem.at[which], recv_sem.at[which],
            2 * high + 1 - core, me,
        ).start()

        def send(i, carry):
            c = partner(me, i)
            for j in range(2):
                copy_to(
                    st_ref.at[c, j], out_ref.at[me, rows], send_sem.at[which], recv_sem.at[which],
                    2 * high + j, c,
                ).start()
            return carry

        lax.fori_loop(1, 64, send, 0)

    def send_filter():
        def turn(g, carry):
            to_pieces(filt_ref, filt_st, g, core, lambda owners: filt_st.at[owners])
            return carry

        lax.fori_loop(0, 4, turn, 0)
        rows = pl.ds(128, 32)
        pltpu.make_async_copy(filt_st.at[me], out_ref.at[me, rows], recv_sem.at[2]).start()

        def send(i, carry):
            c = partner(me, i)
            copy_to(
                filt_st.at[c], out_ref.at[me, rows], send_sem.at[2], recv_sem.at[2], dp, c
            ).start()
            return carry

        lax.fori_loop(1, 64, send, 0)

    send_signal(0, up_ref, up_st)
    send_filter()
    send_signal(1, sig_ref, sig_st)
    for which, rows in ((0, pl.ds(0, 64)), (1, pl.ds(64, 64)), (2, pl.ds(128, 32))):
        wait_bytes(out_ref.at[:, rows], recv_sem.at[which])
    for which, st_ref in ((0, up_st), (1, sig_st)):
        wait_bytes(st_ref.at[pl.ds(0, 63)], send_sem.at[which])
        wait_bytes(st_ref.at[0, 0], send_sem.at[which])
    wait_bytes(filt_st.at[pl.ds(0, 63)], send_sem.at[2])


def scatter_kernel(
    ig_ref, fg_ref, ig_out, fg_out, ig_in, fg_in, total, fg_parts, send_sem, recv_sem
):
    dp = lax.axis_index("dp")
    me = lax.axis_index("ctx")
    core, high = dp % 2, dp // 2
    for step in range(1, 4):
        q = (high + step) % 4
        copy_to(
            fg_ref.at[q], fg_in.at[high], send_sem.at[0], recv_sem.at[0], 2 * q + core, me
        ).start()
    pltpu.make_async_copy(ig_ref.at[me, core], ig_in.at[me, core], recv_sem.at[1]).start()
    copy_to(
        ig_ref.at[me, 1 - core], ig_in.at[me, core], send_sem.at[1], recv_sem.at[1],
        2 * high + 1 - core, me,
    ).start()

    def send(i, carry):
        c = partner(me, i)
        for j in range(2):
            copy_to(
                ig_ref.at[c, j], ig_in.at[me, core], send_sem.at[1], recv_sem.at[1],
                2 * high + j, c,
            ).start()
        return carry

    lax.fori_loop(1, 64, send, 0)
    wait_bytes(fg_in.at[pl.ds(0, 3)], recv_sem.at[0])

    def add(p, carry):
        terms = fg_ref[high, p].astype(jnp.float32)
        for step in range(1, 4):
            terms = terms + fg_in[(high + step) % 4, p].astype(jnp.float32)
        total[2 * p] = terms[0:8]
        total[2 * p + 1] = terms[8:16]
        return carry

    lax.fori_loop(0, 32, add, 0)
    pltpu.make_async_copy(total.at[me], fg_parts.at[me], recv_sem.at[2]).start()

    def send_total(i, carry):
        c = partner(me, i)
        copy_to(total.at[c], fg_parts.at[me], send_sem.at[2], recv_sem.at[2], dp, c).start()
        return carry

    lax.fori_loop(1, 64, send_total, 0)
    wait_bytes(ig_in, recv_sem.at[1])

    def turn(i, carry):
        g, j = i // 2, i % 2
        owners = pl.ds(pl.multiple_of(16 * g, 16), 16)
        block = ig_in[owners, j].astype(jnp.float32)
        for q in range(4):
            cols = pl.ds(pl.multiple_of(512 * (2 * q + j) + 128 * g, 128), 128)
            part = block[:, 8 * q : 8 * q + 8, :].reshape(128, 128)
            ig_out[:, cols] = part.T.astype(jnp.bfloat16)
        return carry

    lax.fori_loop(0, 8, turn, 0)
    wait_bytes(fg_parts, recv_sem.at[2])
    for g in range(4):
        part = fg_parts[pl.ds(16 * g, 16)].reshape(128, 128)
        fg_out[:, pl.ds(128 * g, 128)] = part.T
    wait_bytes(fg_in.at[pl.ds(0, 3)], send_sem.at[0])
    wait_bytes(ig_in.at[pl.ds(0, 63)], send_sem.at[1])
    wait_bytes(ig_in.at[0, 0], send_sem.at[1])
    wait_bytes(fg_parts.at[pl.ds(0, 63)], send_sem.at[2])


def vmem():
    return pl.BlockSpec(memory_space=pltpu.VMEM)


def gather_call(up, sig, filt):
    return pl.pallas_call(
        gather_kernel,
        out_shape=jax.ShapeDtypeStruct((64, 160, 128), jnp.bfloat16),
        in_specs=[vmem()] * 3,
        out_specs=pl.BlockSpec(memory_space=pl.ANY),
        scratch_shapes=[
            pltpu.VMEM((64, 2, 32, 128), jnp.bfloat16),
            pltpu.VMEM((64, 2, 32, 128), jnp.bfloat16),
            pltpu.VMEM((64, 32, 128), jnp.bfloat16),
            pltpu.SemaphoreType.DMA((3,)),
            pltpu.SemaphoreType.DMA((3,)),
        ],
        compiler_params=pltpu.CompilerParams(
            has_side_effects=True, vmem_limit_bytes=32 * 1024 * 1024
        ),
    )(up, sig, filt)


def scatter_call(ig, fg):
    return pl.pallas_call(
        scatter_kernel,
        out_shape=(
            jax.ShapeDtypeStruct((128, 4096), jnp.bfloat16),
            jax.ShapeDtypeStruct((128, 512), jnp.float32),
        ),
        in_specs=[vmem()] * 2,
        out_specs=(vmem(), vmem()),
        scratch_shapes=[
            pltpu.VMEM((64, 2, 32, 128), jnp.bfloat16),
            pltpu.VMEM((4, 32, 16, 128), jnp.bfloat16),
            pltpu.VMEM((64, 8, 128), jnp.float32),
            pltpu.VMEM((64, 8, 128), jnp.float32),
            pltpu.SemaphoreType.DMA((3,)),
            pltpu.SemaphoreType.DMA((3,)),
        ],
        compiler_params=pltpu.CompilerParams(
            has_side_effects=True, vmem_limit_bytes=32 * 1024 * 1024
        ),
    )(ig, fg)


def shards(inputs, grad_out, filt):
    recv = gather_call(grad_out[0], inputs[0], filt)
    ig, fg = compute_call(recv)
    input_grad, filter_grad = scatter_call(ig, fg)
    return input_grad[None], filter_grad


def solution(mesh):
    in_specs = (P("dp", "ctx", None), P("dp", "ctx", None), P("ctx", None))
    out_specs = (P("dp", "ctx", None), P("ctx", "dp"))
    return jax.shard_map(shards, mesh=mesh, in_specs=in_specs, out_specs=out_specs, check_vma=False)
```

```python
import math
import numpy as np
import jax
import jax.numpy as jnp
from jax import lax
from jax.experimental import pallas as pl
from jax.experimental.pallas import tpu as pltpu
from jax.sharding import PartitionSpec as P

N = 16384
KN = 65
KC = 5


def cmul_const(v, c, s):
    re, im = v
    if abs(s) < 1e-12 and abs(c - 1) < 1e-12:
        return v
    if abs(c) < 1e-12 and abs(s - 1) < 1e-12:
        return (-im, re)
    if abs(c) < 1e-12 and abs(s + 1) < 1e-12:
        return (im, -re)
    if abs(abs(c) - abs(s)) < 1e-12:
        h = abs(c)
        sc, ss = (1.0 if c > 0 else -1.0), (1.0 if s > 0 else -1.0)
        a = re * h
        b = im * h
        first = (a if sc > 0 else -a)
        first = first - b if ss > 0 else first + b
        second = (b if sc > 0 else -b)
        second = second + a if ss > 0 else second - a
        return (first, second)
    return (re * c - im * s, re * s + im * c)


def fft_complex(values, sign):
    n = len(values)
    if n == 1:
        return values
    if n == 2:
        (ar, ai), (br, bi) = values
        return [(ar + br, ai + bi), (ar - br, ai - bi)]
    if n % 4 == 0:
        quarter = n // 4
        parts = [fft_complex(values[r::4], sign) for r in range(4)]
        out = [None] * n
        for k in range(quarter):
            turned = []
            for r in range(4):
                angle = sign * 2.0 * math.pi * r * k / n
                turned.append(cmul_const(parts[r][k], math.cos(angle), math.sin(angle)))
            (ar, ai), (br, bi), (cr, ci), (dr, di) = turned
            s0r, s0i, s1r, s1i = ar + cr, ai + ci, ar - cr, ai - ci
            s2r, s2i, s3r, s3i = br + dr, bi + di, br - dr, bi - di
            out[k] = (s0r + s2r, s0i + s2i)
            out[k + 2 * quarter] = (s0r - s2r, s0i - s2i)
            if sign < 0:
                out[k + quarter] = (s1r + s3i, s1i - s3r)
                out[k + 3 * quarter] = (s1r - s3i, s1i + s3r)
            else:
                out[k + quarter] = (s1r - s3i, s1i + s3r)
                out[k + 3 * quarter] = (s1r + s3i, s1i - s3r)
        return out
    half = n // 2
    even = fft_complex(values[0::2], sign)
    odd = fft_complex(values[1::2], sign)
    out = [None] * n
    for k in range(half):
        angle = sign * 2.0 * math.pi * k / n
        tr, ti = cmul_const(odd[k], math.cos(angle), math.sin(angle))
        er, ei = even[k]
        out[k] = (er + tr, ei + ti)
        out[k + half] = (er - tr, ei - ti)
    return out


def odd_bins(values, period):
    quarter = period // 4
    turned = []
    for a in range(quarter):
        angle = -2.0 * math.pi * a / period
        turned.append(cmul_const((values[a], -values[a + quarter]), math.cos(angle), math.sin(angle)))
    spectrum = fft_complex(turned, -1.0)
    found = {}
    for l in range(quarter):
        k = 4 * l + 1
        re, im = spectrum[l]
        if k <= period // 2:
            found[k] = (re, im)
        else:
            found[period - k] = (re, -im)
    return found


def real_bins(values):
    n = len(values)
    if n == 2:
        return {0: (values[0] + values[1], None), 1: (values[0] - values[1], None)}
    half = n // 2
    sums = [values[a] + values[a + half] for a in range(half)]
    diffs = [values[a] - values[a + half] for a in range(half)]
    found = {2 * k: v for k, v in real_bins(sums).items()}
    found.update(odd_bins(diffs, n))
    return found


def padded_bins(values):
    found = odd_bins(values, 2 * len(values))
    found.update({2 * k: v for k, v in real_bins(values).items()})
    return found


def odd_values(bins, period):
    quarter = period // 4
    spectrum = []
    for l in range(quarter):
        k = 4 * l + 1
        if k <= period // 2:
            spectrum.append(bins[k])
        else:
            re, im = bins[period - k]
            spectrum.append((re, -im))
    turned = fft_complex(spectrum, 1.0)
    lower, upper = [], []
    for a in range(quarter):
        angle = 2.0 * math.pi * a / period
        re, im = cmul_const(turned[a], math.cos(angle), math.sin(angle))
        lower.append(re)
        upper.append(-im)
    return lower + upper


def real_values(bins, n):
    if n == 2:
        return [bins[0][0] + bins[1][0], bins[0][0] - bins[1][0]]
    sums = real_values({k // 2: v for k, v in bins.items() if k % 2 == 0}, n // 2)
    diffs = odd_values(bins, n)
    return [s + d for s, d in zip(sums, diffs)] + [s - d for s, d in zip(sums, diffs)]


def padded_values(bins, n):
    odd = odd_values(bins, 2 * n)
    even = real_values({k // 2: v for k, v in bins.items() if k % 2 == 0}, n)
    return [o + e for o, e in zip(odd, even)]


def big_tables():
    m = np.arange(128)
    grid = (m[:, None] * m[None, :] % 128) * (2.0 * np.pi / 128)
    c, s = np.cos(grid), np.sin(grid)
    full = np.block([[c, -s], [s, c]]).astype(np.float32)
    high = full.astype(jnp.bfloat16)
    low = (full - high.astype(np.float32)).astype(jnp.bfloat16)
    turn = np.arange(72)[:, None] * m[None, :] * (2.0 * np.pi / N)
    return high, low, np.cos(turn).astype(np.float32), np.sin(turn).astype(np.float32)


def spectra_of(src_ref, y_ref, first, tr_ref, ti_ref, group):
    rows = pl.ds(pl.multiple_of(group * 16, 16), 16)
    kept = pl.ds(pl.multiple_of(first + group * 16, 16), 16)
    bins = padded_bins([src_ref[a, rows, :].astype(jnp.float32) for a in range(64)])
    for k in range(KN):
        re, im = bins[k]
        tr, ti = tr_ref[pl.ds(k, 1), :], ti_ref[pl.ds(k, 1), :]
        if im is None:
            re, im = re * tr, -(re * ti)
        else:
            re, im = re * tr + im * ti, im * tr - re * ti
        y_ref[k, kept, pl.ds(0, 128)] = re.astype(jnp.bfloat16)
        y_ref[k, kept, pl.ds(128, 128)] = im.astype(jnp.bfloat16)


def forward_dot(y_ref, k0, first, rows, hi_ref, lo_ref):
    y = y_ref[pl.ds(k0, KC), pl.ds(first, rows), :].reshape(KC * rows, 256)
    spec = jnp.dot(y, hi_ref[...], preferred_element_type=jnp.float32)
    spec = spec + jnp.dot(y, lo_ref[...], preferred_element_type=jnp.float32)
    return spec.reshape(KC, rows, 256)


def inverse_dot(prods, hi_ref, lo_ref):
    prod = jnp.concatenate(prods, axis=0)
    form = (((1,), (1,)), ((), ()))
    back = lax.dot_general(prod, hi_ref[...], form, preferred_element_type=jnp.float32)
    back = back + lax.dot_general(prod, lo_ref[...], form, preferred_element_type=jnp.float32)
    return back.reshape(KC, prod.shape[0] // KC, 256)


def conj_product(x, u):
    xr, xi = x[:, :128], x[:, 128:]
    ur, ui = u[:, :128], u[:, 128:]
    return xr * ur + xi * ui, xr * ui - xi * ur


def values_of(v_ref, tr_ref, ti_ref, rows):
    bins = {}
    for k in range(KN):
        re, im = v_ref[k, rows, pl.ds(0, 128)], v_ref[k, rows, pl.ds(128, 128)]
        tr, ti = tr_ref[pl.ds(k, 1), :], ti_ref[pl.ds(k, 1), :]
        if k in (0, 64):
            bins[k] = (re * tr - im * ti, None)
        else:
            bins[k] = (re * tr - im * ti, im * tr + re * ti)
    return padded_values(bins, 64)


def copy_to(src, dst, send_sem, recv_sem, dp, ctx):
    return pltpu.make_async_remote_copy(
        src_ref=src,
        dst_ref=dst,
        send_sem=send_sem,
        recv_sem=recv_sem,
        device_id=(dp, ctx),
        device_id_type=pl.DeviceIdType.MESH,
    )


def wait_bytes(ref, sem):
    pltpu.make_async_copy(ref, ref, sem).wait()


def partner(me, i):
    return ((me // 16 + i % 4) % 4) * 16 + (me % 16 + i // 4) % 16


def to_pieces(x_ref, st_ref, g, j, index):
    parts = []
    for q in range(4):
        cols = pl.ds(pl.multiple_of(512 * (2 * q + j) + 128 * g, 128), 128)
        parts.append(x_ref[:, cols].astype(jnp.float32).T.reshape(16, 8, 128))
    owners = pl.ds(pl.multiple_of(16 * g, 16), 16)
    index(owners)[...] = jnp.concatenate(parts, axis=1).astype(jnp.bfloat16)


def loop(start, stop, step):
    def run(i, carry):
        step(i)
        return carry

    lax.fori_loop(start, stop, run, 0)


def fused_kernel(
    up_hbm, sig_hbm, filt_hbm, hi_ref, lo_ref, tr_ref, ti_ref,
    ig_out, fg_out,
    up_x, sig_x, filt_x, up_st, sig_st, filt_st, up_in, sig_in, filt_in,
    y_ref, u_ref, v_ref, ig_st, fg_st, ig_in, fg_in, total, fg_parts,
    load_sem, send_sem, recv_sem,
):
    dp = lax.axis_index("dp")
    me = lax.axis_index("ctx")
    core, high = dp % 2, dp // 2
    mesh_id = pl.DeviceIdType.MESH
    loads = [
        pltpu.make_async_copy(src, dst, load_sem.at[i])
        for i, (src, dst) in enumerate(((up_hbm, up_x), (sig_hbm, sig_x), (filt_hbm, filt_x)))
    ]
    for load in loads:
        load.start()
    barrier = pltpu.get_barrier_semaphore()
    pl.semaphore_signal(barrier, inc=1, device_id=(2 * high + 1 - core, me), device_id_type=mesh_id)
    for step in range(1, 4):
        pl.semaphore_signal(
            barrier, inc=1, device_id=(2 * ((high + step) % 4) + core, me), device_id_type=mesh_id
        )

    def greet(i):
        c = partner(me, i)
        for j in range(2):
            pl.semaphore_signal(barrier, inc=1, device_id=(2 * high + j, c), device_id_type=mesh_id)

    loop(1, 64, greet)

    def turn_signal(x_ref, st_ref):
        def turn(i):
            g, j = i // 2, i % 2
            to_pieces(x_ref, st_ref, g, j, lambda owners: st_ref.at[owners, j])

        loop(0, 8, turn)

    def spread(src_ref, dst_ref, slot, which):
        pltpu.make_async_copy(src_ref.at[me, core], dst_ref.at[slot], recv_sem.at[which]).start()
        copy_to(
            src_ref.at[me, 1 - core], dst_ref.at[slot], send_sem.at[which], recv_sem.at[which],
            2 * high + 1 - core, me,
        ).start()

        def send(i):
            c = partner(me, i)
            for j in range(2):
                copy_to(
                    src_ref.at[c, j], dst_ref.at[slot], send_sem.at[which], recv_sem.at[which],
                    2 * high + j, c,
                ).start()

        loop(1, 64, send)

    def spread_same(src_ref, dst_ref, which):
        pltpu.make_async_copy(src_ref.at[me], dst_ref.at[me], recv_sem.at[which]).start()

        def send(i):
            c = partner(me, i)
            copy_to(
                src_ref.at[c], dst_ref.at[me], send_sem.at[which], recv_sem.at[which], dp, c
            ).start()

        loop(1, 64, send)

    loads[0].wait()
    turn_signal(up_x, up_st)
    pl.semaphore_wait(barrier, 130)
    mine = (me, pl.ds(pl.multiple_of(32 * core, 32), 32))
    spread(up_st, up_in, mine, 0)
    loads[1].wait()
    turn_signal(sig_x, sig_st)
    spread(sig_st, sig_in, mine, 1)
    loads[2].wait()
    loop(0, 4, lambda g: to_pieces(filt_x, filt_st, g, core, lambda owners: filt_st.at[owners]))
    spread_same(filt_st, filt_in, 2)

    wait_bytes(up_in, recv_sem.at[0])
    loop(0, 4, lambda g: spectra_of(up_in, y_ref, 0, tr_ref, ti_ref, g))

    def up_spectra(step):
        k0 = step * KC
        spec = forward_dot(y_ref, k0, 0, 64, hi_ref, lo_ref)
        for i in range(KC):
            k = k0 + i
            scale = jnp.where((k == 0) | (k == 64), 1.0 / N, 2.0 / N).astype(jnp.float32)
            u_ref[k] = spec[i] * scale

    loop(0, KN // KC, up_spectra)

    wait_bytes(sig_in, recv_sem.at[1])
    loop(0, 4, lambda g: spectra_of(sig_in, y_ref, 64, tr_ref, ti_ref, g))

    def filter_products(step):
        k0 = step * KC
        spec = forward_dot(y_ref, k0, 64, 64, hi_ref, lo_ref)
        prods = []
        for i in range(KC):
            re, im = conj_product(spec[i], u_ref[k0 + i])
            re, im = re[0:32] + re[32:64], im[0:32] + im[32:64]
            prods.append(jnp.concatenate([re, im], axis=1).astype(jnp.bfloat16))
        v_ref[pl.ds(k0, KC), pl.ds(64, 32), :] = inverse_dot(prods, hi_ref, lo_ref)

    loop(0, KN // KC, filter_products)

    def filter_values(group):
        rows = pl.ds(pl.multiple_of(64 + group * 16, 16), 16)
        out = values_of(v_ref, tr_ref, ti_ref, rows)
        for a in range(0, 64, 2):
            for h in range(2):
                pair = jnp.concatenate([out[a][8 * h:8 * h + 8], out[a + 1][8 * h:8 * h + 8]], axis=0)
                fg_st[2 * group + h, a // 2, :, :] = pair.astype(jnp.bfloat16)

    loop(0, 2, filter_values)
    for step in range(1, 4):
        q = (high + step) % 4
        copy_to(fg_st.at[q], fg_in.at[high], send_sem.at[3], recv_sem.at[3], 2 * q + core, me).start()

    wait_bytes(filt_in, recv_sem.at[2])
    loop(0, 2, lambda g: spectra_of(filt_in, y_ref, 128, tr_ref, ti_ref, g))

    def input_products(step):
        k0 = step * KC
        spec = forward_dot(y_ref, k0, 128, 32, hi_ref, lo_ref)
        prods = []
        for i in range(KC):
            both = jnp.concatenate([spec[i], spec[i]], axis=0)
            re, im = conj_product(both, u_ref[k0 + i])
            prods.append(jnp.concatenate([re, im], axis=1).astype(jnp.bfloat16))
        v_ref[pl.ds(k0, KC), pl.ds(0, 64), :] = inverse_dot(prods, hi_ref, lo_ref)

    loop(0, KN // KC, input_products)

    def input_values(group):
        rows = pl.ds(pl.multiple_of(group * 16, 16), 16)
        out = values_of(v_ref, tr_ref, ti_ref, rows)
        kept = pl.ds(pl.multiple_of((group % 2) * 16, 16), 16)
        for a in range(64):
            ig_st[a, group // 2, kept, :] = out[a].astype(jnp.bfloat16)

    loop(0, 4, input_values)
    spread(ig_st, ig_in, (me, core), 4)

    wait_bytes(fg_in.at[pl.ds(0, 3)], recv_sem.at[3])

    def add(p):
        terms = fg_st[high, p].astype(jnp.float32)
        for step in range(1, 4):
            terms = terms + fg_in[(high + step) % 4, p].astype(jnp.float32)
        total[2 * p] = terms[0:8]
        total[2 * p + 1] = terms[8:16]

    loop(0, 32, add)
    spread_same(total, fg_parts, 5)
    wait_bytes(ig_in, recv_sem.at[4])

    def turn_back(i):
        g, j = i // 2, i % 2
        owners = pl.ds(pl.multiple_of(16 * g, 16), 16)
        block = ig_in[owners, j].astype(jnp.float32)
        for q in range(4):
            cols = pl.ds(pl.multiple_of(512 * (2 * q + j) + 128 * g, 128), 128)
            part = block[:, 8 * q : 8 * q + 8, :].reshape(128, 128)
            ig_out[:, cols] = part.T.astype(jnp.bfloat16)

    loop(0, 8, turn_back)
    wait_bytes(fg_parts, recv_sem.at[5])
    for g in range(4):
        part = fg_parts[pl.ds(16 * g, 16)].reshape(128, 128)
        fg_out[:, pl.ds(128 * g, 128)] = part.T
    for which in (0, 1, 4):
        wait_bytes(ig_in.at[pl.ds(0, 63)], send_sem.at[which])
        wait_bytes(ig_in.at[0, 0], send_sem.at[which])
    wait_bytes(filt_in.at[pl.ds(0, 63)], send_sem.at[2])
    wait_bytes(fg_in.at[pl.ds(0, 3)], send_sem.at[3])
    wait_bytes(fg_parts.at[pl.ds(0, 63)], send_sem.at[5])


def shards(inputs, grad_out, filt):
    vmem = pl.BlockSpec(memory_space=pltpu.VMEM)
    hbm = pl.BlockSpec(memory_space=pl.ANY)
    tables = [jnp.asarray(t) for t in big_tables()]
    bf16, f32 = jnp.bfloat16, jnp.float32
    input_grad, filter_grad = pl.pallas_call(
        fused_kernel,
        out_shape=(
            jax.ShapeDtypeStruct((128, 4096), bf16),
            jax.ShapeDtypeStruct((128, 512), f32),
        ),
        in_specs=[hbm] * 3 + [vmem] * 4,
        out_specs=(vmem, vmem),
        scratch_shapes=[
            pltpu.VMEM((128, 4096), bf16),
            pltpu.VMEM((128, 4096), bf16),
            pltpu.VMEM((128, 4096), bf16),
            pltpu.VMEM((64, 2, 32, 128), bf16),
            pltpu.VMEM((64, 2, 32, 128), bf16),
            pltpu.VMEM((64, 32, 128), bf16),
            pltpu.VMEM((64, 64, 128), bf16),
            pltpu.VMEM((64, 64, 128), bf16),
            pltpu.VMEM((64, 32, 128), bf16),
            pltpu.VMEM((KN, 160, 256), bf16),
            pltpu.VMEM((KN, 64, 256), f32),
            pltpu.VMEM((KN, 96, 256), f32),
            pltpu.VMEM((64, 2, 32, 128), bf16),
            pltpu.VMEM((4, 32, 16, 128), bf16),
            pltpu.VMEM((64, 2, 32, 128), bf16),
            pltpu.VMEM((4, 32, 16, 128), bf16),
            pltpu.VMEM((64, 8, 128), f32),
            pltpu.VMEM((64, 8, 128), f32),
            pltpu.SemaphoreType.DMA((3,)),
            pltpu.SemaphoreType.DMA((6,)),
            pltpu.SemaphoreType.DMA((6,)),
        ],
        compiler_params=pltpu.CompilerParams(
            collective_id=0, has_side_effects=True, vmem_limit_bytes=50 * 1024 * 1024
        ),
    )(grad_out[0], inputs[0], filt, *tables)
    return input_grad[None], filter_grad


def solution(mesh):
    in_specs = (P("dp", "ctx", None), P("dp", "ctx", None), P("ctx", None))
    out_specs = (P("dp", "ctx", None), P("ctx", "dp"))
    return jax.shard_map(shards, mesh=mesh, in_specs=in_specs, out_specs=out_specs, check_vma=False)
```

```python
import math
import numpy as np
import jax
import jax.numpy as jnp
from jax import lax
from jax.experimental import pallas as pl
from jax.experimental.pallas import tpu as pltpu
from jax.sharding import PartitionSpec as P

N = 16384
KN = 65
KC = 5


def cmul_const(v, c, s):
    re, im = v
    if abs(s) < 1e-12 and abs(c - 1) < 1e-12:
        return v
    if abs(c) < 1e-12 and abs(s - 1) < 1e-12:
        return (-im, re)
    if abs(c) < 1e-12 and abs(s + 1) < 1e-12:
        return (im, -re)
    if abs(abs(c) - abs(s)) < 1e-12:
        h = abs(c)
        sc, ss = (1.0 if c > 0 else -1.0), (1.0 if s > 0 else -1.0)
        a = re * h
        b = im * h
        first = (a if sc > 0 else -a)
        first = first - b if ss > 0 else first + b
        second = (b if sc > 0 else -b)
        second = second + a if ss > 0 else second - a
        return (first, second)
    return (re * c - im * s, re * s + im * c)


def fft_complex(values, sign):
    n = len(values)
    if n == 1:
        return values
    if n == 2:
        (ar, ai), (br, bi) = values
        return [(ar + br, ai + bi), (ar - br, ai - bi)]
    if n % 4 == 0:
        quarter = n // 4
        parts = [fft_complex(values[r::4], sign) for r in range(4)]
        out = [None] * n
        for k in range(quarter):
            turned = []
            for r in range(4):
                angle = sign * 2.0 * math.pi * r * k / n
                turned.append(cmul_const(parts[r][k], math.cos(angle), math.sin(angle)))
            (ar, ai), (br, bi), (cr, ci), (dr, di) = turned
            s0r, s0i, s1r, s1i = ar + cr, ai + ci, ar - cr, ai - ci
            s2r, s2i, s3r, s3i = br + dr, bi + di, br - dr, bi - di
            out[k] = (s0r + s2r, s0i + s2i)
            out[k + 2 * quarter] = (s0r - s2r, s0i - s2i)
            if sign < 0:
                out[k + quarter] = (s1r + s3i, s1i - s3r)
                out[k + 3 * quarter] = (s1r - s3i, s1i + s3r)
            else:
                out[k + quarter] = (s1r - s3i, s1i + s3r)
                out[k + 3 * quarter] = (s1r + s3i, s1i - s3r)
        return out
    half = n // 2
    even = fft_complex(values[0::2], sign)
    odd = fft_complex(values[1::2], sign)
    out = [None] * n
    for k in range(half):
        angle = sign * 2.0 * math.pi * k / n
        tr, ti = cmul_const(odd[k], math.cos(angle), math.sin(angle))
        er, ei = even[k]
        out[k] = (er + tr, ei + ti)
        out[k + half] = (er - tr, ei - ti)
    return out


def odd_bins(values, period):
    quarter = period // 4
    turned = []
    for a in range(quarter):
        angle = -2.0 * math.pi * a / period
        turned.append(cmul_const((values[a], -values[a + quarter]), math.cos(angle), math.sin(angle)))
    spectrum = fft_complex(turned, -1.0)
    found = {}
    for l in range(quarter):
        k = 4 * l + 1
        re, im = spectrum[l]
        if k <= period // 2:
            found[k] = (re, im)
        else:
            found[period - k] = (re, -im)
    return found


def real_bins(values):
    n = len(values)
    if n == 2:
        return {0: (values[0] + values[1], None), 1: (values[0] - values[1], None)}
    half = n // 2
    sums = [values[a] + values[a + half] for a in range(half)]
    diffs = [values[a] - values[a + half] for a in range(half)]
    found = {2 * k: v for k, v in real_bins(sums).items()}
    found.update(odd_bins(diffs, n))
    return found


def padded_bins(values):
    found = odd_bins(values, 2 * len(values))
    found.update({2 * k: v for k, v in real_bins(values).items()})
    return found


def odd_values(bins, period):
    quarter = period // 4
    spectrum = []
    for l in range(quarter):
        k = 4 * l + 1
        if k <= period // 2:
            spectrum.append(bins[k])
        else:
            re, im = bins[period - k]
            spectrum.append((re, -im))
    turned = fft_complex(spectrum, 1.0)
    lower, upper = [], []
    for a in range(quarter):
        angle = 2.0 * math.pi * a / period
        re, im = cmul_const(turned[a], math.cos(angle), math.sin(angle))
        lower.append(re)
        upper.append(-im)
    return lower + upper


def real_values(bins, n):
    if n == 2:
        return [bins[0][0] + bins[1][0], bins[0][0] - bins[1][0]]
    sums = real_values({k // 2: v for k, v in bins.items() if k % 2 == 0}, n // 2)
    diffs = odd_values(bins, n)
    return [s + d for s, d in zip(sums, diffs)] + [s - d for s, d in zip(sums, diffs)]


def padded_values(bins, n):
    odd = odd_values(bins, 2 * n)
    even = real_values({k // 2: v for k, v in bins.items() if k % 2 == 0}, n)
    return [o + e for o, e in zip(odd, even)]


def big_tables():
    m = np.arange(128)
    grid = (m[:, None] * m[None, :] % 128) * (2.0 * np.pi / 128)
    c, s = np.cos(grid), np.sin(grid)
    full = np.block([[c, -s], [s, c]]).astype(np.float32)
    high = full.astype(jnp.bfloat16)
    low = (full - high.astype(np.float32)).astype(jnp.bfloat16)
    turn = np.arange(72)[:, None] * m[None, :] * (2.0 * np.pi / N)
    return np.stack([high, low]), np.stack([np.cos(turn), np.sin(turn)]).astype(np.float32)


def spectra_of(src_ref, y_ref, first, tw_ref, group):
    rows = pl.ds(pl.multiple_of(group * 16, 16), 16)
    kept = pl.ds(pl.multiple_of(first + group * 16, 16), 16)
    bins = padded_bins([src_ref[a, rows, :].astype(jnp.float32) for a in range(64)])
    for k in range(KN):
        re, im = bins[k]
        tr, ti = tw_ref[0, pl.ds(k, 1), :], tw_ref[1, pl.ds(k, 1), :]
        if im is None:
            re, im = re * tr, -(re * ti)
        else:
            re, im = re * tr + im * ti, im * tr - re * ti
        y_ref[k, kept, pl.ds(0, 128)] = re.astype(jnp.bfloat16)
        y_ref[k, kept, pl.ds(128, 128)] = im.astype(jnp.bfloat16)


def forward_dot(y_ref, k0, first, rows, tab_ref):
    y = y_ref[pl.ds(k0, KC), pl.ds(first, rows), :].reshape(KC * rows, 256)
    spec = jnp.dot(y, tab_ref[0], preferred_element_type=jnp.float32)
    spec = spec + jnp.dot(y, tab_ref[1], preferred_element_type=jnp.float32)
    return spec.reshape(KC, rows, 256)


def inverse_dot(prods, tab_ref):
    prod = jnp.concatenate(prods, axis=0)
    form = (((1,), (1,)), ((), ()))
    back = lax.dot_general(prod, tab_ref[0], form, preferred_element_type=jnp.float32)
    back = back + lax.dot_general(prod, tab_ref[1], form, preferred_element_type=jnp.float32)
    return back.reshape(KC, prod.shape[0] // KC, 256)


def conj_product(x, u):
    xr, xi = x[:, :128], x[:, 128:]
    ur, ui = u[:, :128], u[:, 128:]
    return xr * ur + xi * ui, xr * ui - xi * ur


def values_of(v_ref, tw_ref, rows):
    bins = {}
    for k in range(KN):
        re, im = v_ref[k, rows, pl.ds(0, 128)], v_ref[k, rows, pl.ds(128, 128)]
        tr, ti = tw_ref[0, pl.ds(k, 1), :], tw_ref[1, pl.ds(k, 1), :]
        if k in (0, 64):
            bins[k] = (re * tr - im * ti, None)
        else:
            bins[k] = (re * tr - im * ti, im * tr + re * ti)
    return padded_values(bins, 64)


def copy_to(src, dst, send_sem, recv_sem, dp, ctx):
    return pltpu.make_async_remote_copy(
        src_ref=src,
        dst_ref=dst,
        send_sem=send_sem,
        recv_sem=recv_sem,
        device_id=(dp, ctx),
        device_id_type=pl.DeviceIdType.MESH,
    )


def wait_bytes(ref, sem):
    pltpu.make_async_copy(ref, ref, sem).wait()


def partner(me, i):
    return ((me // 16 + i % 4) % 4) * 16 + (me % 16 + i // 4) % 16


def to_pieces(x_ref, st_ref, g, j, index):
    parts = []
    for q in range(4):
        cols = pl.ds(pl.multiple_of(512 * (2 * q + j) + 128 * g, 128), 128)
        parts.append(x_ref[:, cols].astype(jnp.float32).T.reshape(16, 8, 128))
    owners = pl.ds(pl.multiple_of(16 * g, 16), 16)
    index(owners)[...] = jnp.concatenate(parts, axis=1).astype(jnp.bfloat16)


def loop(start, stop, step):
    def run(i, carry):
        step(i)
        return carry

    lax.fori_loop(start, stop, run, 0)


def fused_kernel(
    up_hbm, sig_hbm, filt_hbm, tab_hbm, tw_hbm,
    ig_out, fg_out,
    tab_ref, tw_ref,
    up_x, sig_x, filt_x, up_st, sig_st, filt_st, up_in, sig_in, filt_in,
    y_ref, u_ref, v_ref, ig_st, fg_st, ig_in, fg_in, fg_mid, fg_last, total, fg_parts,
    load_sem, send_sem, recv_sem,
):
    dp = lax.axis_index("dp")
    me = lax.axis_index("ctx")
    core, high = dp % 2, dp // 2
    plane, place = me // 16, me % 16
    mesh_id = pl.DeviceIdType.MESH

    def owner(cube, c):
        odd = cube % 2
        z = c // 16
        return 16 * (odd * z + (1 - odd) * (3 - z)) + c % 16

    mine = owner(high, me)
    late = mine // 32
    flip, mirror = high + 1 - 2 * (high % 2), 3 - high
    first_cube = (1 - late) * flip + late * mirror
    second_cube = (1 - late) * mirror + late * flip
    far_cube = 3 - flip
    reflected = (3 - plane) * 16 + place

    loads = [
        pltpu.make_async_copy(src, dst, load_sem.at[i])
        for i, (src, dst) in enumerate(
            (
                (up_hbm, up_x), (filt_hbm, filt_x), (sig_hbm, sig_x),
                (tab_hbm, tab_ref), (tw_hbm, tw_ref),
            )
        )
    ]
    for load in loads:
        load.start()
    barrier = pltpu.get_barrier_semaphore()

    def hail(there, c):
        pl.semaphore_signal(barrier, inc=1, device_id=(there, c), device_id_type=mesh_id)

    hail(2 * high + 1 - core, me)
    hail(2 * first_cube + core, reflected)
    hail(2 * second_cube + core, reflected)

    def greet(i):
        c = partner(me, i)
        for j in range(2):
            hail(2 * high + j, c)

    loop(1, 64, greet)

    def greet_outside(i):
        step = i // 16
        lower = 1 - plane // 2
        z = lower * (-1 - step) + (1 - lower) * (4 + step)
        there = (high + z // 4 + 4) % 4
        hail(2 * there + core, (z % 4) * 16 + (place + i) % 16)

    outer = 1 - (plane % 3 + 1) // 2
    loop(0, 16 * (1 + outer), greet_outside)

    def turn_signal(x_ref, st_ref):
        def turn(i):
            g, j = i // 2, i % 2
            to_pieces(x_ref, st_ref, g, j, lambda owners: st_ref.at[owners, j])

        loop(0, 8, turn)

    def spread(src_ref, piece, dst_ref, slot, which):
        here = piece(me)
        pltpu.make_async_copy(src_ref.at[here, core], dst_ref.at[slot], recv_sem.at[which]).start()
        copy_to(
            src_ref.at[here, 1 - core], dst_ref.at[slot], send_sem.at[which], recv_sem.at[which],
            2 * high + 1 - core, me,
        ).start()

        def send(i):
            c = partner(me, i)
            for j in range(2):
                copy_to(
                    src_ref.at[piece(c), j], dst_ref.at[slot], send_sem.at[which],
                    recv_sem.at[which], 2 * high + j, c,
                ).start()

        loop(1, 64, send)

    def spread_filter():
        pltpu.make_async_copy(filt_st.at[mine], filt_in.at[me], recv_sem.at[2]).start()

        def send(i):
            there = (place + i // 4) % 16
            even = 1 - (there // 4 + there % 4) % 2
            ahead = i % 4
            step = ahead - 4 * (ahead // 3) - 4 * (1 - even) * (1 - ahead % 2) * (ahead // 2)
            z = (4 * high + plane + step + 16) % 16
            cube = z // 4
            c = (z % 4) * 16 + there
            copy_to(
                filt_st.at[owner(cube, c)], filt_in.at[me], send_sem.at[2], recv_sem.at[2],
                2 * cube + core, c,
            ).start()

        loop(1, 64, send)

    def spread_total():
        pltpu.make_async_copy(total.at[me], fg_parts.at[mine], recv_sem.at[5]).start()

        def send(i):
            c = partner(me, i)
            copy_to(
                total.at[c], fg_parts.at[mine], send_sem.at[5], recv_sem.at[5], dp, c
            ).start()

        loop(1, 64, send)

    loads[0].wait()
    turn_signal(up_x, up_st)
    pl.semaphore_wait(barrier, 129 + 16 * (1 + outer))
    rows = pl.ds(pl.multiple_of(32 * core, 32), 32)
    spread(up_st, lambda c: owner(high, c), up_in, (me, rows), 0)
    loads[1].wait()
    loop(0, 4, lambda g: to_pieces(filt_x, filt_st, g, core, lambda owners: filt_st.at[owners]))
    spread_filter()
    loads[2].wait()
    turn_signal(sig_x, sig_st)
    spread(sig_st, lambda c: owner(high, c), sig_in, (me, rows), 1)
    loads[3].wait()
    loads[4].wait()

    wait_bytes(up_in, recv_sem.at[0])
    loop(0, 4, lambda g: spectra_of(up_in, y_ref, 0, tw_ref, g))

    def up_spectra(step):
        k0 = step * KC
        spec = forward_dot(y_ref, k0, 0, 64, tab_ref)
        for i in range(KC):
            k = k0 + i
            scale = jnp.where((k == 0) | (k == 64), 1.0 / N, 2.0 / N).astype(jnp.float32)
            u_ref[k] = spec[i] * scale

    loop(0, KN // KC, up_spectra)

    wait_bytes(filt_in, recv_sem.at[2])
    loop(0, 2, lambda g: spectra_of(filt_in, y_ref, 128, tw_ref, g))

    def input_products(step):
        k0 = step * KC
        spec = forward_dot(y_ref, k0, 128, 32, tab_ref)
        prods = []
        for i in range(KC):
            both = jnp.concatenate([spec[i], spec[i]], axis=0)
            re, im = conj_product(both, u_ref[k0 + i])
            prods.append(jnp.concatenate([re, im], axis=1).astype(jnp.bfloat16))
        v_ref[pl.ds(k0, KC), pl.ds(0, 64), :] = inverse_dot(prods, tab_ref)

    loop(0, KN // KC, input_products)

    def input_values(group):
        rows = pl.ds(pl.multiple_of(group * 16, 16), 16)
        out = values_of(v_ref, tw_ref, rows)
        kept = pl.ds(pl.multiple_of((group % 2) * 16, 16), 16)
        for a in range(64):
            ig_st[a, group // 2, kept, :] = out[a].astype(jnp.bfloat16)

    loop(0, 4, input_values)
    spread(ig_st, lambda c: c, ig_in, (mine, core), 4)

    wait_bytes(sig_in, recv_sem.at[1])
    loop(0, 4, lambda g: spectra_of(sig_in, y_ref, 64, tw_ref, g))

    def filter_products(step):
        k0 = step * KC
        spec = forward_dot(y_ref, k0, 64, 64, tab_ref)
        prods = []
        for i in range(KC):
            re, im = conj_product(spec[i], u_ref[k0 + i])
            re, im = re[0:32] + re[32:64], im[0:32] + im[32:64]
            prods.append(jnp.concatenate([re, im], axis=1).astype(jnp.bfloat16))
        v_ref[pl.ds(k0, KC), pl.ds(64, 32), :] = inverse_dot(prods, tab_ref)

    loop(0, KN // KC, filter_products)

    def filter_values(group):
        rows = pl.ds(pl.multiple_of(64 + group * 16, 16), 16)
        out = values_of(v_ref, tw_ref, rows)
        for a in range(0, 64, 2):
            for h in range(2):
                pair = jnp.concatenate([out[a][8 * h:8 * h + 8], out[a + 1][8 * h:8 * h + 8]], axis=0)
                fg_st[2 * group + h, a // 2, :, :] = pair.astype(jnp.bfloat16)

    loop(0, 2, filter_values)
    copy_to(
        fg_st.at[first_cube], fg_in.at[0], send_sem.at[3], recv_sem.at[3],
        2 * first_cube + core, reflected,
    ).start()
    copy_to(
        fg_st.at[far_cube], fg_in.at[1], send_sem.at[3], recv_sem.at[3],
        2 * first_cube + core, reflected,
    ).start()

    wait_bytes(fg_in, recv_sem.at[3])

    def add_half(p):
        terms = fg_st[second_cube, p].astype(jnp.float32) + fg_in[1, p].astype(jnp.float32)
        fg_mid[p] = terms.astype(jnp.bfloat16)

    loop(0, 32, add_half)
    copy_to(
        fg_mid, fg_last, send_sem.at[6], recv_sem.at[6], 2 * second_cube + core, reflected
    ).start()
    wait_bytes(fg_last, recv_sem.at[6])

    def add_last(p):
        terms = fg_st[high, p].astype(jnp.float32) + fg_in[0, p].astype(jnp.float32)
        terms = terms + fg_last[p].astype(jnp.float32)
        total[2 * p] = terms[0:8]
        total[2 * p + 1] = terms[8:16]

    loop(0, 32, add_last)
    spread_total()
    wait_bytes(ig_in, recv_sem.at[4])

    def turn_back(i):
        g, j = i // 2, i % 2
        owners = pl.ds(pl.multiple_of(16 * g, 16), 16)
        block = ig_in[owners, j].astype(jnp.float32)
        for q in range(4):
            cols = pl.ds(pl.multiple_of(512 * (2 * q + j) + 128 * g, 128), 128)
            part = block[:, 8 * q : 8 * q + 8, :].reshape(128, 128)
            ig_out[:, cols] = part.T.astype(jnp.bfloat16)

    loop(0, 8, turn_back)
    wait_bytes(fg_parts, recv_sem.at[5])
    for g in range(4):
        part = fg_parts[pl.ds(16 * g, 16)].reshape(128, 128)
        fg_out[:, pl.ds(128 * g, 128)] = part.T
    for which in (0, 1, 4):
        wait_bytes(ig_in.at[pl.ds(0, 63)], send_sem.at[which])
        wait_bytes(ig_in.at[0, 0], send_sem.at[which])
    wait_bytes(filt_in.at[pl.ds(0, 63)], send_sem.at[2])
    wait_bytes(fg_in, send_sem.at[3])
    wait_bytes(fg_mid, send_sem.at[6])
    wait_bytes(fg_parts.at[pl.ds(0, 63)], send_sem.at[5])


def shards(inputs, grad_out, filt):
    vmem = pl.BlockSpec(memory_space=pltpu.VMEM)
    hbm = pl.BlockSpec(memory_space=pl.ANY)
    tables = [jnp.asarray(t) for t in big_tables()]
    bf16, f32 = jnp.bfloat16, jnp.float32
    input_grad, filter_grad = pl.pallas_call(
        fused_kernel,
        out_shape=(
            jax.ShapeDtypeStruct((128, 4096), bf16),
            jax.ShapeDtypeStruct((128, 512), f32),
        ),
        in_specs=[hbm] * 5,
        out_specs=(vmem, vmem),
        scratch_shapes=[
            pltpu.VMEM((2, 256, 256), bf16),
            pltpu.VMEM((2, 72, 128), f32),
            pltpu.VMEM((128, 4096), bf16),
            pltpu.VMEM((128, 4096), bf16),
            pltpu.VMEM((128, 4096), bf16),
            pltpu.VMEM((64, 2, 32, 128), bf16),
            pltpu.VMEM((64, 2, 32, 128), bf16),
            pltpu.VMEM((64, 32, 128), bf16),
            pltpu.VMEM((64, 64, 128), bf16),
            pltpu.VMEM((64, 64, 128), bf16),
            pltpu.VMEM((64, 32, 128), bf16),
            pltpu.VMEM((KN, 160, 256), bf16),
            pltpu.VMEM((KN, 64, 256), f32),
            pltpu.VMEM((KN, 96, 256), f32),
            pltpu.VMEM((64, 2, 32, 128), bf16),
            pltpu.VMEM((4, 32, 16, 128), bf16),
            pltpu.VMEM((64, 2, 32, 128), bf16),
            pltpu.VMEM((2, 32, 16, 128), bf16),
            pltpu.VMEM((32, 16, 128), bf16),
            pltpu.VMEM((32, 16, 128), bf16),
            pltpu.VMEM((64, 8, 128), f32),
            pltpu.VMEM((64, 8, 128), f32),
            pltpu.SemaphoreType.DMA((5,)),
            pltpu.SemaphoreType.DMA((7,)),
            pltpu.SemaphoreType.DMA((7,)),
        ],
        compiler_params=pltpu.CompilerParams(
            collective_id=0, has_side_effects=True, vmem_limit_bytes=60 * 1024 * 1024
        ),
    )(grad_out[0], inputs[0], filt, *tables)
    return input_grad[None], filter_grad


def solution(mesh):
    in_specs = (P("dp", "ctx", None), P("dp", "ctx", None), P("ctx", None))
    out_specs = (P("dp", "ctx", None), P("ctx", "dp"))
    return jax.shard_map(shards, mesh=mesh, in_specs=in_specs, out_specs=out_specs, check_vma=False)
```

```python
import math
import numpy as np
import jax
import jax.numpy as jnp
from jax import lax
from jax.experimental import pallas as pl
from jax.experimental.pallas import tpu as pltpu
from jax.sharding import PartitionSpec as P

N = 16384
KN = 65
KC = 5
BACK_A, BACK_B = 24, 44
QUARTERS = (0, 2, 1, 3)


def cmul_const(v, c, s):
    re, im = v
    if abs(s) < 1e-12 and abs(c - 1) < 1e-12:
        return v
    if abs(c) < 1e-12 and abs(s - 1) < 1e-12:
        return (-im, re)
    if abs(c) < 1e-12 and abs(s + 1) < 1e-12:
        return (im, -re)
    if abs(abs(c) - abs(s)) < 1e-12:
        h = abs(c)
        sc, ss = (1.0 if c > 0 else -1.0), (1.0 if s > 0 else -1.0)
        a = re * h
        b = im * h
        first = (a if sc > 0 else -a)
        first = first - b if ss > 0 else first + b
        second = (b if sc > 0 else -b)
        second = second + a if ss > 0 else second - a
        return (first, second)
    return (re * c - im * s, re * s + im * c)


def fft_complex(values, sign):
    n = len(values)
    if n == 1:
        return values
    if n == 2:
        (ar, ai), (br, bi) = values
        return [(ar + br, ai + bi), (ar - br, ai - bi)]
    if n % 4 == 0:
        quarter = n // 4
        parts = [fft_complex(values[r::4], sign) for r in range(4)]
        out = [None] * n
        for k in range(quarter):
            turned = []
            for r in range(4):
                angle = sign * 2.0 * math.pi * r * k / n
                turned.append(cmul_const(parts[r][k], math.cos(angle), math.sin(angle)))
            (ar, ai), (br, bi), (cr, ci), (dr, di) = turned
            s0r, s0i, s1r, s1i = ar + cr, ai + ci, ar - cr, ai - ci
            s2r, s2i, s3r, s3i = br + dr, bi + di, br - dr, bi - di
            out[k] = (s0r + s2r, s0i + s2i)
            out[k + 2 * quarter] = (s0r - s2r, s0i - s2i)
            if sign < 0:
                out[k + quarter] = (s1r + s3i, s1i - s3r)
                out[k + 3 * quarter] = (s1r - s3i, s1i + s3r)
            else:
                out[k + quarter] = (s1r - s3i, s1i + s3r)
                out[k + 3 * quarter] = (s1r + s3i, s1i - s3r)
        return out
    half = n // 2
    even = fft_complex(values[0::2], sign)
    odd = fft_complex(values[1::2], sign)
    out = [None] * n
    for k in range(half):
        angle = sign * 2.0 * math.pi * k / n
        tr, ti = cmul_const(odd[k], math.cos(angle), math.sin(angle))
        er, ei = even[k]
        out[k] = (er + tr, ei + ti)
        out[k + half] = (er - tr, ei - ti)
    return out


def odd_bins(values, period):
    quarter = period // 4
    turned = []
    for a in range(quarter):
        angle = -2.0 * math.pi * a / period
        turned.append(cmul_const((values[a], -values[a + quarter]), math.cos(angle), math.sin(angle)))
    spectrum = fft_complex(turned, -1.0)
    found = {}
    for l in range(quarter):
        k = 4 * l + 1
        re, im = spectrum[l]
        if k <= period // 2:
            found[k] = (re, im)
        else:
            found[period - k] = (re, -im)
    return found


def real_bins(values):
    n = len(values)
    if n == 2:
        return {0: (values[0] + values[1], None), 1: (values[0] - values[1], None)}
    half = n // 2
    sums = [values[a] + values[a + half] for a in range(half)]
    diffs = [values[a] - values[a + half] for a in range(half)]
    found = {2 * k: v for k, v in real_bins(sums).items()}
    found.update(odd_bins(diffs, n))
    return found


def padded_bins(values):
    found = odd_bins(values, 2 * len(values))
    found.update({2 * k: v for k, v in real_bins(values).items()})
    return found


def odd_values(bins, period):
    quarter = period // 4
    spectrum = []
    for l in range(quarter):
        k = 4 * l + 1
        if k <= period // 2:
            spectrum.append(bins[k])
        else:
            re, im = bins[period - k]
            spectrum.append((re, -im))
    turned = fft_complex(spectrum, 1.0)
    lower, upper = [], []
    for a in range(quarter):
        angle = 2.0 * math.pi * a / period
        re, im = cmul_const(turned[a], math.cos(angle), math.sin(angle))
        lower.append(re)
        upper.append(-im)
    return lower + upper


def real_values(bins, n):
    if n == 2:
        return [bins[0][0] + bins[1][0], bins[0][0] - bins[1][0]]
    sums = real_values({k // 2: v for k, v in bins.items() if k % 2 == 0}, n // 2)
    diffs = odd_values(bins, n)
    return [s + d for s, d in zip(sums, diffs)] + [s - d for s, d in zip(sums, diffs)]


def padded_values(bins, n):
    odd = odd_values(bins, 2 * n)
    even = real_values({k // 2: v for k, v in bins.items() if k % 2 == 0}, n)
    return [o + e for o, e in zip(odd, even)]


def big_tables():
    m = np.arange(128)
    grid = (m[:, None] * m[None, :] % 128) * (2.0 * np.pi / 128)
    c, s = np.cos(grid), np.sin(grid)
    full = np.block([[c, -s], [s, c]]).astype(np.float32)
    high = full.astype(jnp.bfloat16)
    low = (full - high.astype(np.float32)).astype(jnp.bfloat16)
    turn = np.arange(72)[:, None] * m[None, :] * (2.0 * np.pi / N)
    return np.stack([high, low]), np.stack([np.cos(turn), np.sin(turn)]).astype(np.float32)


def spectra_of(src_ref, y_ref, tw_ref, group, place):
    rows = pl.ds(pl.multiple_of(group * 16, 16), 16)
    kept = pl.ds(pl.multiple_of(place * 16, 16), 16)
    bins = padded_bins([src_ref[a, rows, :].astype(jnp.float32) for a in range(64)])
    for k in range(KN):
        re, im = bins[k]
        tr, ti = tw_ref[0, pl.ds(k, 1), :], tw_ref[1, pl.ds(k, 1), :]
        if im is None:
            re, im = re * tr, -(re * ti)
        else:
            re, im = re * tr + im * ti, im * tr - re * ti
        y_ref[k, kept, pl.ds(0, 128)] = re.astype(jnp.bfloat16)
        y_ref[k, kept, pl.ds(128, 128)] = im.astype(jnp.bfloat16)


def forward_dot(y_ref, k0, first, rows, tab_ref):
    y = y_ref[pl.ds(k0, KC), pl.ds(first, rows), :].reshape(KC * rows, 256)
    spec = jnp.dot(y, tab_ref[0], preferred_element_type=jnp.float32)
    spec = spec + jnp.dot(y, tab_ref[1], preferred_element_type=jnp.float32)
    return spec.reshape(KC, rows, 256)


def inverse_dot(prods, tab_ref):
    prod = jnp.concatenate(prods, axis=0)
    form = (((1,), (1,)), ((), ()))
    back = lax.dot_general(prod, tab_ref[0], form, preferred_element_type=jnp.float32)
    back = back + lax.dot_general(prod, tab_ref[1], form, preferred_element_type=jnp.float32)
    return back.reshape(KC, prod.shape[0] // KC, 256)


def conj_product(x, u):
    xr, xi = x[:, :128], x[:, 128:]
    ur, ui = u[:, :128], u[:, 128:]
    return xr * ur + xi * ui, xr * ui - xi * ur


def values_of(v_ref, tw_ref, rows):
    bins = {}
    for k in range(KN):
        re, im = v_ref[k, rows, pl.ds(0, 128)], v_ref[k, rows, pl.ds(128, 128)]
        tr, ti = tw_ref[0, pl.ds(k, 1), :], tw_ref[1, pl.ds(k, 1), :]
        if k in (0, 64):
            bins[k] = (re * tr - im * ti, None)
        else:
            bins[k] = (re * tr - im * ti, im * tr + re * ti)
    return padded_values(bins, 64)


def copy_to(src, dst, send_sem, recv_sem, dp, ctx):
    return pltpu.make_async_remote_copy(
        src_ref=src,
        dst_ref=dst,
        send_sem=send_sem,
        recv_sem=recv_sem,
        device_id=(dp, ctx),
        device_id_type=pl.DeviceIdType.MESH,
    )


def wait_bytes(ref, sem):
    pltpu.make_async_copy(ref, ref, sem).wait()


def partner(me, i):
    return ((me // 16 + i % 4) % 4) * 16 + (me % 16 + i // 4) % 16


def to_pieces(x_ref, st_ref, g, j, index):
    parts = []
    for q in QUARTERS:
        cols = pl.ds(pl.multiple_of(512 * (2 * q + j) + 128 * g, 128), 128)
        parts.append(x_ref[:, cols].astype(jnp.float32).T.reshape(16, 8, 128))
    owners = pl.ds(pl.multiple_of(16 * g, 16), 16)
    index(owners)[...] = jnp.concatenate(parts, axis=1).astype(jnp.bfloat16)


def loop(start, stop, step):
    def run(i, carry):
        step(i)
        return carry

    lax.fori_loop(start, stop, run, 0)


def fused_kernel(
    up_hbm, sig_hbm, filt_hbm, tab_hbm, tw_hbm,
    ig_out, fg_out,
    tab_ref, tw_ref,
    up_x, sig_x, filt_x, up_st, sig_st, filt_st, up_in, sig_in, filt_in,
    y_ref, u_ref, v_ref, ig_st, fg_st, ig_in, fg_in, fg_mid, fg_last, total, fg_parts,
    load_sem, send_sem, recv_sem,
):
    dp = lax.axis_index("dp")
    me = lax.axis_index("ctx")
    core, high = dp % 2, dp // 2
    plane, place = me // 16, me % 16
    mesh_id = pl.DeviceIdType.MESH

    def owner(cube, c):
        odd = cube % 2
        z = c // 16
        return 16 * (odd * z + (1 - odd) * (3 - z)) + c % 16

    mine = owner(high, me)
    late = mine // 32
    flip, mirror = high + 1 - 2 * (high % 2), 3 - high
    first_cube = (1 - late) * flip + late * mirror
    second_cube = (1 - late) * mirror + late * flip
    far_cube = 3 - flip
    reflected = (3 - plane) * 16 + place

    loads = [
        pltpu.make_async_copy(src, dst, load_sem.at[i])
        for i, (src, dst) in enumerate(
            (
                (up_hbm, up_x), (filt_hbm, filt_x), (sig_hbm, sig_x),
                (tab_hbm, tab_ref), (tw_hbm, tw_ref),
            )
        )
    ]
    for load in loads:
        load.start()
    barrier = pltpu.get_barrier_semaphore()

    def hail(there, c):
        pl.semaphore_signal(barrier, inc=1, device_id=(there, c), device_id_type=mesh_id)

    hail(2 * high + 1 - core, me)
    hail(2 * first_cube + core, reflected)
    hail(2 * second_cube + core, reflected)

    def greet(i):
        c = partner(me, i)
        for j in range(2):
            hail(2 * high + j, c)

    loop(1, 64, greet)

    def greet_outside(i):
        step = i // 16
        lower = 1 - plane // 2
        z = lower * (-1 - step) + (1 - lower) * (4 + step)
        there = (high + z // 4 + 4) % 4
        hail(2 * there + core, (z % 4) * 16 + (place + i) % 16)

    outer = 1 - (plane % 3 + 1) // 2
    loop(0, 16 * (1 + outer), greet_outside)

    def turn_signal(x_ref, st_ref):
        def turn(i):
            g, j = i // 2, i % 2
            to_pieces(x_ref, st_ref, g, j, lambda owners: st_ref.at[owners, j])

        loop(0, 8, turn)

    def spread(src_ref, piece, dst_ref, slot, which):
        def begin():
            here = piece(me)
            pltpu.make_async_copy(
                src_ref.at[here, core], dst_ref.at[slot], recv_sem.at[which]
            ).start()
            copy_to(
                src_ref.at[here, 1 - core], dst_ref.at[slot], send_sem.at[which],
                recv_sem.at[which], 2 * high + 1 - core, me,
            ).start()

        def send(i):
            c = partner(me, i)
            for j in range(2):
                copy_to(
                    src_ref.at[piece(c), j], dst_ref.at[slot], send_sem.at[which],
                    recv_sem.at[which], 2 * high + j, c,
                ).start()

        return begin, send

    def spread_all(*args):
        begin, send = spread(*args)
        begin()
        loop(1, 64, send)

    def send_signal_half(half):
        part = pl.ds(16 * half, 16)
        slot = (me, pl.ds(pl.multiple_of(32 * core + 16 * half, 16), 16))
        sems = send_sem.at[7 + half], recv_sem.at[7 + half]
        pltpu.make_async_copy(sig_st.at[mine, core, part], sig_in.at[slot], sems[1]).start()
        copy_to(
            sig_st.at[mine, 1 - core, part], sig_in.at[slot], *sems, 2 * high + 1 - core, me
        ).start()

        def send(i):
            c = partner(me, i)
            for j in range(2):
                copy_to(
                    sig_st.at[owner(high, c), j, part], sig_in.at[slot], *sems, 2 * high + j, c
                ).start()

        loop(1, 64, send)

    def spread_filter():
        pltpu.make_async_copy(filt_st.at[mine], filt_in.at[me], recv_sem.at[2]).start()

        def send(i):
            there = (place + i // 4) % 16
            even = 1 - (there // 4 + there % 4) % 2
            ahead = i % 4
            step = ahead - 4 * (ahead // 3) - 4 * (1 - even) * (1 - ahead % 2) * (ahead // 2)
            z = (4 * high + plane + step + 16) % 16
            cube = z // 4
            c = (z % 4) * 16 + there
            copy_to(
                filt_st.at[owner(cube, c)], filt_in.at[me], send_sem.at[2], recv_sem.at[2],
                2 * cube + core, c,
            ).start()

        loop(1, 64, send)

    def spread_total():
        pltpu.make_async_copy(total.at[me], fg_parts.at[mine], recv_sem.at[5]).start()

        def send(i):
            c = partner(me, i)
            copy_to(
                total.at[c], fg_parts.at[mine], send_sem.at[5], recv_sem.at[5], dp, c
            ).start()

        loop(1, 64, send)

    loads[0].wait()
    turn_signal(up_x, up_st)
    pl.semaphore_wait(barrier, 129 + 16 * (1 + outer))
    rows = pl.ds(pl.multiple_of(32 * core, 32), 32)
    spread_all(up_st, lambda c: owner(high, c), up_in, (me, rows), 0)
    loads[1].wait()
    loop(0, 4, lambda g: to_pieces(filt_x, filt_st, g, core, lambda owners: filt_st.at[owners]))
    spread_filter()
    loads[2].wait()
    turn_signal(sig_x, sig_st)
    for half in range(2):
        send_signal_half(half)
    loads[3].wait()
    loads[4].wait()

    wait_bytes(up_in, recv_sem.at[0])
    loop(0, 4, lambda g: spectra_of(up_in, y_ref, tw_ref, g, g))

    def up_spectra(step):
        k0 = step * KC
        spec = forward_dot(y_ref, k0, 0, 64, tab_ref)
        for i in range(KC):
            k = k0 + i
            scale = jnp.where((k == 0) | (k == 64), 1.0 / N, 2.0 / N).astype(jnp.float32)
            u_ref[k] = spec[i] * scale

    loop(0, KN // KC, up_spectra)

    wait_bytes(filt_in, recv_sem.at[2])
    loop(0, 2, lambda g: spectra_of(filt_in, y_ref, tw_ref, g, 8 + g))

    def input_products(step):
        k0 = step * KC
        spec = forward_dot(y_ref, k0, 128, 32, tab_ref)
        prods = []
        for i in range(KC):
            both = jnp.concatenate([spec[i], spec[i]], axis=0)
            re, im = conj_product(both, u_ref[k0 + i])
            prods.append(jnp.concatenate([re, im], axis=1).astype(jnp.bfloat16))
        v_ref[pl.ds(k0, KC), pl.ds(0, 64), :] = inverse_dot(prods, tab_ref)

    loop(0, KN // KC, input_products)

    def input_values(group):
        rows = pl.ds(pl.multiple_of(group * 16, 16), 16)
        out = values_of(v_ref, tw_ref, rows)
        kept = pl.ds(pl.multiple_of((group % 2) * 16, 16), 16)
        for a in range(64):
            ig_st[a, group // 2, kept, :] = out[a].astype(jnp.bfloat16)

    loop(0, 4, input_values)
    begin_back, send_back = spread(ig_st, lambda c: c, ig_in, (mine, core), 4)
    begin_back()
    loop(1, BACK_A, send_back)

    def filter_half(half):
        wait_bytes(sig_in.at[:, pl.ds(0, 32)], recv_sem.at[7 + half])
        loop(0, 2, lambda g: spectra_of(sig_in, y_ref, tw_ref, 2 * g + half, 4 + 2 * half + g))
        first_row = pl.multiple_of(64 + 32 * half, 32)
        above = pl.ds(pl.multiple_of(16 * half, 16), 16)
        below = pl.ds(pl.multiple_of(32 + 16 * half, 16), 16)
        rows = pl.ds(pl.multiple_of(64 + 16 * half, 16), 16)

        def filter_products(step):
            k0 = step * KC
            spec = forward_dot(y_ref, k0, first_row, 32, tab_ref)
            prods = []
            for i in range(KC):
                u = jnp.concatenate([u_ref[k0 + i, above, :], u_ref[k0 + i, below, :]], axis=0)
                re, im = conj_product(spec[i], u)
                re, im = re[0:16] + re[16:32], im[0:16] + im[16:32]
                prods.append(jnp.concatenate([re, im], axis=1).astype(jnp.bfloat16))
            v_ref[pl.ds(k0, KC), rows, :] = inverse_dot(prods, tab_ref)

        loop(0, KN // KC, filter_products)
        out = values_of(v_ref, tw_ref, rows)
        for a in range(0, 64, 2):
            for h in range(2):
                pair = jnp.concatenate([out[a][8 * h:8 * h + 8], out[a + 1][8 * h:8 * h + 8]], axis=0)
                fg_st[half + 2 * h, a // 2, :, :] = pair.astype(jnp.bfloat16)
        far = half * (high % 2) + (1 - half) * (1 - high % 2)
        copy_to(
            fg_st.at[far * far_cube + (1 - far) * first_cube], fg_in.at[far],
            send_sem.at[9 + far], recv_sem.at[9 + far], 2 * first_cube + core, reflected,
        ).start()

    loop(0, 2, filter_half)

    loop(BACK_A, BACK_B, send_back)
    wait_bytes(fg_in.at[1], recv_sem.at[10])

    def add_half(p):
        terms = fg_st[second_cube, p].astype(jnp.float32) + fg_in[1, p].astype(jnp.float32)
        fg_mid[p] = terms.astype(jnp.bfloat16)

    loop(0, 32, add_half)
    copy_to(
        fg_mid, fg_last, send_sem.at[6], recv_sem.at[6], 2 * second_cube + core, reflected
    ).start()
    loop(BACK_B, 64, send_back)
    wait_bytes(fg_last, recv_sem.at[6])
    wait_bytes(fg_in.at[0], recv_sem.at[9])

    def add_last(p):
        terms = fg_st[high, p].astype(jnp.float32) + fg_in[0, p].astype(jnp.float32)
        terms = terms + fg_last[p].astype(jnp.float32)
        total[2 * p] = terms[0:8]
        total[2 * p + 1] = terms[8:16]

    loop(0, 32, add_last)
    spread_total()
    wait_bytes(ig_in, recv_sem.at[4])

    def turn_back(i):
        g, j = i // 2, i % 2
        owners = pl.ds(pl.multiple_of(16 * g, 16), 16)
        block = ig_in[owners, j].astype(jnp.float32)
        for at, q in enumerate(QUARTERS):
            cols = pl.ds(pl.multiple_of(512 * (2 * q + j) + 128 * g, 128), 128)
            part = block[:, 8 * at : 8 * at + 8, :].reshape(128, 128)
            ig_out[:, cols] = part.T.astype(jnp.bfloat16)

    loop(0, 8, turn_back)
    wait_bytes(fg_parts, recv_sem.at[5])
    for g in range(4):
        part = fg_parts[pl.ds(16 * g, 16)].reshape(128, 128)
        fg_out[:, pl.ds(128 * g, 128)] = part.T
    for which in (7, 8):
        wait_bytes(sig_in.at[pl.ds(0, 63), pl.ds(0, 32)], send_sem.at[which])
        wait_bytes(sig_in.at[0, pl.ds(0, 16)], send_sem.at[which])
    for which in (0, 4):
        wait_bytes(ig_in.at[pl.ds(0, 63)], send_sem.at[which])
        wait_bytes(ig_in.at[0, 0], send_sem.at[which])
    wait_bytes(filt_in.at[pl.ds(0, 63)], send_sem.at[2])
    wait_bytes(fg_in.at[0], send_sem.at[9])
    wait_bytes(fg_in.at[1], send_sem.at[10])
    wait_bytes(fg_mid, send_sem.at[6])
    wait_bytes(fg_parts.at[pl.ds(0, 63)], send_sem.at[5])


def shards(inputs, grad_out, filt):
    vmem = pl.BlockSpec(memory_space=pltpu.VMEM)
    hbm = pl.BlockSpec(memory_space=pl.ANY)
    tables = [jnp.asarray(t) for t in big_tables()]
    bf16, f32 = jnp.bfloat16, jnp.float32
    input_grad, filter_grad = pl.pallas_call(
        fused_kernel,
        out_shape=(
            jax.ShapeDtypeStruct((128, 4096), bf16),
            jax.ShapeDtypeStruct((128, 512), f32),
        ),
        in_specs=[hbm] * 5,
        out_specs=(vmem, vmem),
        scratch_shapes=[
            pltpu.VMEM((2, 256, 256), bf16),
            pltpu.VMEM((2, 72, 128), f32),
            pltpu.VMEM((128, 4096), bf16),
            pltpu.VMEM((128, 4096), bf16),
            pltpu.VMEM((128, 4096), bf16),
            pltpu.VMEM((64, 2, 32, 128), bf16),
            pltpu.VMEM((64, 2, 32, 128), bf16),
            pltpu.VMEM((64, 32, 128), bf16),
            pltpu.VMEM((64, 64, 128), bf16),
            pltpu.VMEM((64, 64, 128), bf16),
            pltpu.VMEM((64, 32, 128), bf16),
            pltpu.VMEM((KN, 160, 256), bf16),
            pltpu.VMEM((KN, 64, 256), f32),
            pltpu.VMEM((KN, 96, 256), f32),
            pltpu.VMEM((64, 2, 32, 128), bf16),
            pltpu.VMEM((4, 32, 16, 128), bf16),
            pltpu.VMEM((64, 2, 32, 128), bf16),
            pltpu.VMEM((2, 32, 16, 128), bf16),
            pltpu.VMEM((32, 16, 128), bf16),
            pltpu.VMEM((32, 16, 128), bf16),
            pltpu.VMEM((64, 8, 128), f32),
            pltpu.VMEM((64, 8, 128), f32),
            pltpu.SemaphoreType.DMA((5,)),
            pltpu.SemaphoreType.DMA((11,)),
            pltpu.SemaphoreType.DMA((11,)),
        ],
        compiler_params=pltpu.CompilerParams(
            collective_id=0, has_side_effects=True, vmem_limit_bytes=60 * 1024 * 1024
        ),
    )(grad_out[0], inputs[0], filt, *tables)
    return input_grad[None], filter_grad


def solution(mesh):
    in_specs = (P("dp", "ctx", None), P("dp", "ctx", None), P("ctx", None))
    out_specs = (P("dp", "ctx", None), P("ctx", "dp"))
    return jax.shard_map(shards, mesh=mesh, in_specs=in_specs, out_specs=out_specs, check_vma=False)
```

```python
import math
import numpy as np
import jax
import jax.numpy as jnp
from jax import lax
from jax.experimental import pallas as pl
from jax.experimental.pallas import tpu as pltpu
from jax.sharding import PartitionSpec as P

N = 16384
KN = 65
KC = 13
BACK_A, BACK_B = 24, 44
QUARTERS = (0, 2, 1, 3)


def cmul_const(v, c, s):
    re, im = v
    if abs(s) < 1e-12 and abs(c - 1) < 1e-12:
        return v
    if abs(c) < 1e-12 and abs(s - 1) < 1e-12:
        return (-im, re)
    if abs(c) < 1e-12 and abs(s + 1) < 1e-12:
        return (im, -re)
    if abs(abs(c) - abs(s)) < 1e-12:
        h = abs(c)
        sc, ss = (1.0 if c > 0 else -1.0), (1.0 if s > 0 else -1.0)
        a = re * h
        b = im * h
        first = (a if sc > 0 else -a)
        first = first - b if ss > 0 else first + b
        second = (b if sc > 0 else -b)
        second = second + a if ss > 0 else second - a
        return (first, second)
    return (re * c - im * s, re * s + im * c)


def fft_complex(values, sign):
    n = len(values)
    if n == 1:
        return values
    if n == 2:
        (ar, ai), (br, bi) = values
        return [(ar + br, ai + bi), (ar - br, ai - bi)]
    if n % 4 == 0:
        quarter = n // 4
        parts = [fft_complex(values[r::4], sign) for r in range(4)]
        out = [None] * n
        for k in range(quarter):
            turned = []
            for r in range(4):
                angle = sign * 2.0 * math.pi * r * k / n
                turned.append(cmul_const(parts[r][k], math.cos(angle), math.sin(angle)))
            (ar, ai), (br, bi), (cr, ci), (dr, di) = turned
            s0r, s0i, s1r, s1i = ar + cr, ai + ci, ar - cr, ai - ci
            s2r, s2i, s3r, s3i = br + dr, bi + di, br - dr, bi - di
            out[k] = (s0r + s2r, s0i + s2i)
            out[k + 2 * quarter] = (s0r - s2r, s0i - s2i)
            if sign < 0:
                out[k + quarter] = (s1r + s3i, s1i - s3r)
                out[k + 3 * quarter] = (s1r - s3i, s1i + s3r)
            else:
                out[k + quarter] = (s1r - s3i, s1i + s3r)
                out[k + 3 * quarter] = (s1r + s3i, s1i - s3r)
        return out
    half = n // 2
    even = fft_complex(values[0::2], sign)
    odd = fft_complex(values[1::2], sign)
    out = [None] * n
    for k in range(half):
        angle = sign * 2.0 * math.pi * k / n
        tr, ti = cmul_const(odd[k], math.cos(angle), math.sin(angle))
        er, ei = even[k]
        out[k] = (er + tr, ei + ti)
        out[k + half] = (er - tr, ei - ti)
    return out


def odd_bins(values, period):
    quarter = period // 4
    turned = []
    for a in range(quarter):
        angle = -2.0 * math.pi * a / period
        turned.append(cmul_const((values[a], -values[a + quarter]), math.cos(angle), math.sin(angle)))
    spectrum = fft_complex(turned, -1.0)
    found = {}
    for l in range(quarter):
        k = 4 * l + 1
        re, im = spectrum[l]
        if k <= period // 2:
            found[k] = (re, im)
        else:
            found[period - k] = (re, -im)
    return found


def real_bins(values):
    n = len(values)
    if n == 2:
        return {0: (values[0] + values[1], None), 1: (values[0] - values[1], None)}
    half = n // 2
    sums = [values[a] + values[a + half] for a in range(half)]
    diffs = [values[a] - values[a + half] for a in range(half)]
    found = {2 * k: v for k, v in real_bins(sums).items()}
    found.update(odd_bins(diffs, n))
    return found


def padded_bins(values):
    found = odd_bins(values, 2 * len(values))
    found.update({2 * k: v for k, v in real_bins(values).items()})
    return found


def odd_values(bins, period):
    quarter = period // 4
    spectrum = []
    for l in range(quarter):
        k = 4 * l + 1
        if k <= period // 2:
            spectrum.append(bins[k])
        else:
            re, im = bins[period - k]
            spectrum.append((re, -im))
    turned = fft_complex(spectrum, 1.0)
    lower, upper = [], []
    for a in range(quarter):
        angle = 2.0 * math.pi * a / period
        re, im = cmul_const(turned[a], math.cos(angle), math.sin(angle))
        lower.append(re)
        upper.append(-im)
    return lower + upper


def real_values(bins, n):
    if n == 2:
        return [bins[0][0] + bins[1][0], bins[0][0] - bins[1][0]]
    sums = real_values({k // 2: v for k, v in bins.items() if k % 2 == 0}, n // 2)
    diffs = odd_values(bins, n)
    return [s + d for s, d in zip(sums, diffs)] + [s - d for s, d in zip(sums, diffs)]


def padded_values(bins, n):
    odd = odd_values(bins, 2 * n)
    even = real_values({k // 2: v for k, v in bins.items() if k % 2 == 0}, n)
    return [o + e for o, e in zip(odd, even)]


def big_tables():
    m = np.arange(128)
    grid = (m[:, None] * m[None, :] % 128) * (2.0 * np.pi / 128)
    c, s = np.cos(grid), np.sin(grid)
    full = np.block([[c, -s], [s, c]]).astype(np.float32)
    high = full.astype(jnp.bfloat16)
    low = (full - high.astype(np.float32)).astype(jnp.bfloat16)
    turn = np.arange(72)[:, None] * m[None, :] * (2.0 * np.pi / N)
    return np.stack([high, low]), np.stack([np.cos(turn), np.sin(turn)]).astype(np.float32)


def spectra_of(src_ref, y_ref, tw_ref, group, place):
    rows = pl.ds(pl.multiple_of(group * 16, 16), 16)
    kept = pl.ds(pl.multiple_of(place * 16, 16), 16)
    bins = padded_bins([src_ref[a, rows, :].astype(jnp.float32) for a in range(64)])
    for k in range(KN):
        re, im = bins[k]
        tr, ti = tw_ref[0, pl.ds(k, 1), :], tw_ref[1, pl.ds(k, 1), :]
        if im is None:
            re, im = re * tr, -(re * ti)
        else:
            re, im = re * tr + im * ti, im * tr - re * ti
        y_ref[k, kept, pl.ds(0, 128)] = re.astype(jnp.bfloat16)
        y_ref[k, kept, pl.ds(128, 128)] = im.astype(jnp.bfloat16)


def forward_dot(y_ref, k0, first, rows, tab_ref):
    y = y_ref[pl.ds(k0, KC), pl.ds(first, rows), :].reshape(KC * rows, 256)
    spec = jnp.dot(y, tab_ref[0], preferred_element_type=jnp.float32)
    spec = spec + jnp.dot(y, tab_ref[1], preferred_element_type=jnp.float32)
    return spec.reshape(KC, rows, 256)


def inverse_dot(prods, tab_ref):
    prod = jnp.concatenate(prods, axis=0)
    form = (((1,), (1,)), ((), ()))
    back = lax.dot_general(prod, tab_ref[0], form, preferred_element_type=jnp.float32)
    back = back + lax.dot_general(prod, tab_ref[1], form, preferred_element_type=jnp.float32)
    return back.reshape(KC, prod.shape[0] // KC, 256)


def conj_product(x, u):
    xr, xi = x[:, :128], x[:, 128:]
    ur, ui = u[:, :128], u[:, 128:]
    return xr * ur + xi * ui, xr * ui - xi * ur


def values_of(v_ref, tw_ref, rows):
    bins = {}
    for k in range(KN):
        re, im = v_ref[k, rows, pl.ds(0, 128)], v_ref[k, rows, pl.ds(128, 128)]
        tr, ti = tw_ref[0, pl.ds(k, 1), :], tw_ref[1, pl.ds(k, 1), :]
        if k in (0, 64):
            bins[k] = (re * tr - im * ti, None)
        else:
            bins[k] = (re * tr - im * ti, im * tr + re * ti)
    return padded_values(bins, 64)


def copy_to(src, dst, send_sem, recv_sem, dp, ctx):
    return pltpu.make_async_remote_copy(
        src_ref=src,
        dst_ref=dst,
        send_sem=send_sem,
        recv_sem=recv_sem,
        device_id=(dp, ctx),
        device_id_type=pl.DeviceIdType.MESH,
    )


def wait_bytes(ref, sem):
    pltpu.make_async_copy(ref, ref, sem).wait()


def partner(me, i):
    return ((me // 16 + i % 4) % 4) * 16 + (me % 16 + i // 4) % 16


def to_pieces(x_ref, st_ref, g, j, index):
    parts = []
    for q in QUARTERS:
        cols = pl.ds(pl.multiple_of(512 * (2 * q + j) + 128 * g, 128), 128)
        parts.append(x_ref[:, cols].astype(jnp.float32).T.reshape(16, 8, 128))
    owners = pl.ds(pl.multiple_of(16 * g, 16), 16)
    index(owners)[...] = jnp.concatenate(parts, axis=1).astype(jnp.bfloat16)


def loop(start, stop, step):
    def run(i, carry):
        step(i)
        return carry

    lax.fori_loop(start, stop, run, 0)


def fused_kernel(
    up_hbm, sig_hbm, filt_hbm, tab_hbm, tw_hbm,
    ig_out, fg_out,
    tab_ref, tw_ref,
    up_x, sig_x, filt_x, up_st, sig_st, filt_st, up_in, sig_in, filt_in,
    y_ref, u_ref, v_ref, ig_st, fg_st, ig_in, fg_in, fg_mid, fg_last, total, fg_parts,
    load_sem, send_sem, recv_sem,
):
    dp = lax.axis_index("dp")
    me = lax.axis_index("ctx")
    core, high = dp % 2, dp // 2
    plane, place = me // 16, me % 16
    mesh_id = pl.DeviceIdType.MESH

    def owner(cube, c):
        odd = cube % 2
        z = c // 16
        return 16 * (odd * z + (1 - odd) * (3 - z)) + c % 16

    mine = owner(high, me)
    late = mine // 32
    flip, mirror = high + 1 - 2 * (high % 2), 3 - high
    first_cube = (1 - late) * flip + late * mirror
    second_cube = (1 - late) * mirror + late * flip
    far_cube = 3 - flip
    reflected = (3 - plane) * 16 + place

    loads = [
        pltpu.make_async_copy(src, dst, load_sem.at[i])
        for i, (src, dst) in enumerate(
            (
                (up_hbm, up_x), (filt_hbm, filt_x), (sig_hbm, sig_x),
                (tab_hbm, tab_ref), (tw_hbm, tw_ref),
            )
        )
    ]
    for load in loads:
        load.start()
    barrier = pltpu.get_barrier_semaphore()

    def hail(there, c):
        pl.semaphore_signal(barrier, inc=1, device_id=(there, c), device_id_type=mesh_id)

    hail(2 * high + 1 - core, me)
    hail(2 * first_cube + core, reflected)
    hail(2 * second_cube + core, reflected)

    def greet(i):
        c = partner(me, i)
        for j in range(2):
            hail(2 * high + j, c)

    loop(1, 64, greet)

    def greet_outside(i):
        step = i // 16
        lower = 1 - plane // 2
        z = lower * (-1 - step) + (1 - lower) * (4 + step)
        there = (high + z // 4 + 4) % 4
        hail(2 * there + core, (z % 4) * 16 + (place + i) % 16)

    outer = 1 - (plane % 3 + 1) // 2
    loop(0, 16 * (1 + outer), greet_outside)

    def turn_signal(x_ref, st_ref):
        def turn(i):
            g, j = i // 2, i % 2
            to_pieces(x_ref, st_ref, g, j, lambda owners: st_ref.at[owners, j])

        loop(0, 8, turn)

    def spread(src_ref, piece, dst_ref, slot, which):
        def begin():
            here = piece(me)
            pltpu.make_async_copy(
                src_ref.at[here, core], dst_ref.at[slot], recv_sem.at[which]
            ).start()
            copy_to(
                src_ref.at[here, 1 - core], dst_ref.at[slot], send_sem.at[which],
                recv_sem.at[which], 2 * high + 1 - core, me,
            ).start()

        def send(i):
            c = partner(me, i)
            for j in range(2):
                copy_to(
                    src_ref.at[piece(c), j], dst_ref.at[slot], send_sem.at[which],
                    recv_sem.at[which], 2 * high + j, c,
                ).start()

        return begin, send

    def spread_all(*args):
        begin, send = spread(*args)
        begin()
        loop(1, 64, send)

    def send_signal_half(half):
        part = pl.ds(16 * half, 16)
        slot = (me, pl.ds(pl.multiple_of(32 * core + 16 * half, 16), 16))
        sems = send_sem.at[7 + half], recv_sem.at[7 + half]
        pltpu.make_async_copy(sig_st.at[mine, core, part], sig_in.at[slot], sems[1]).start()
        copy_to(
            sig_st.at[mine, 1 - core, part], sig_in.at[slot], *sems, 2 * high + 1 - core, me
        ).start()

        def send(i):
            c = partner(me, i)
            for j in range(2):
                copy_to(
                    sig_st.at[owner(high, c), j, part], sig_in.at[slot], *sems, 2 * high + j, c
                ).start()

        loop(1, 64, send)

    def spread_filter():
        pltpu.make_async_copy(filt_st.at[mine], filt_in.at[me], recv_sem.at[2]).start()

        def send(i):
            there = (place + i // 4) % 16
            even = 1 - (there // 4 + there % 4) % 2
            ahead = i % 4
            step = ahead - 4 * (ahead // 3) - 4 * (1 - even) * (1 - ahead % 2) * (ahead // 2)
            z = (4 * high + plane + step + 16) % 16
            cube = z // 4
            c = (z % 4) * 16 + there
            copy_to(
                filt_st.at[owner(cube, c)], filt_in.at[me], send_sem.at[2], recv_sem.at[2],
                2 * cube + core, c,
            ).start()

        loop(1, 64, send)

    def spread_total():
        pltpu.make_async_copy(total.at[me], fg_parts.at[mine], recv_sem.at[5]).start()

        def send(i):
            c = partner(me, i)
            copy_to(
                total.at[c], fg_parts.at[mine], send_sem.at[5], recv_sem.at[5], dp, c
            ).start()

        loop(1, 64, send)

    loads[0].wait()
    turn_signal(up_x, up_st)
    pl.semaphore_wait(barrier, 129 + 16 * (1 + outer))
    rows = pl.ds(pl.multiple_of(32 * core, 32), 32)
    spread_all(up_st, lambda c: owner(high, c), up_in, (me, rows), 0)
    loads[1].wait()
    loop(0, 4, lambda g: to_pieces(filt_x, filt_st, g, core, lambda owners: filt_st.at[owners]))
    spread_filter()
    loads[2].wait()
    turn_signal(sig_x, sig_st)
    for half in range(2):
        send_signal_half(half)
    loads[3].wait()
    loads[4].wait()

    wait_bytes(up_in, recv_sem.at[0])
    loop(0, 4, lambda g: spectra_of(up_in, y_ref, tw_ref, g, g))

    def up_spectra(step):
        k0 = step * KC
        spec = forward_dot(y_ref, k0, 0, 64, tab_ref)
        for i in range(KC):
            k = k0 + i
            scale = jnp.where((k == 0) | (k == 64), 1.0 / N, 2.0 / N).astype(jnp.float32)
            u_ref[k] = spec[i] * scale

    loop(0, KN // KC, up_spectra)

    wait_bytes(filt_in, recv_sem.at[2])
    loop(0, 2, lambda g: spectra_of(filt_in, y_ref, tw_ref, g, 8 + g))

    def input_products(step):
        k0 = step * KC
        spec = forward_dot(y_ref, k0, 128, 32, tab_ref)
        prods = []
        for i in range(KC):
            both = jnp.concatenate([spec[i], spec[i]], axis=0)
            re, im = conj_product(both, u_ref[k0 + i])
            prods.append(jnp.concatenate([re, im], axis=1).astype(jnp.bfloat16))
        v_ref[pl.ds(k0, KC), pl.ds(0, 64), :] = inverse_dot(prods, tab_ref)

    loop(0, KN // KC, input_products)

    def input_values(group):
        rows = pl.ds(pl.multiple_of(group * 16, 16), 16)
        out = values_of(v_ref, tw_ref, rows)
        kept = pl.ds(pl.multiple_of((group % 2) * 16, 16), 16)
        for a in range(64):
            ig_st[a, group // 2, kept, :] = out[a].astype(jnp.bfloat16)

    loop(0, 4, input_values)
    begin_back, send_back = spread(ig_st, lambda c: c, ig_in, (mine, core), 4)
    begin_back()
    loop(1, BACK_A, send_back)

    def filter_half(half):
        wait_bytes(sig_in.at[:, pl.ds(0, 32)], recv_sem.at[7 + half])
        loop(0, 2, lambda g: spectra_of(sig_in, y_ref, tw_ref, 2 * g + half, 4 + 2 * half + g))
        first_row = pl.multiple_of(64 + 32 * half, 32)
        above = pl.ds(pl.multiple_of(16 * half, 16), 16)
        below = pl.ds(pl.multiple_of(32 + 16 * half, 16), 16)
        rows = pl.ds(pl.multiple_of(64 + 16 * half, 16), 16)

        def filter_products(step):
            k0 = step * KC
            spec = forward_dot(y_ref, k0, first_row, 32, tab_ref)
            prods = []
            for i in range(KC):
                u = jnp.concatenate([u_ref[k0 + i, above, :], u_ref[k0 + i, below, :]], axis=0)
                re, im = conj_product(spec[i], u)
                re, im = re[0:16] + re[16:32], im[0:16] + im[16:32]
                prods.append(jnp.concatenate([re, im], axis=1).astype(jnp.bfloat16))
            v_ref[pl.ds(k0, KC), rows, :] = inverse_dot(prods, tab_ref)

        loop(0, KN // KC, filter_products)
        out = values_of(v_ref, tw_ref, rows)
        for a in range(0, 64, 2):
            for h in range(2):
                pair = jnp.concatenate([out[a][8 * h:8 * h + 8], out[a + 1][8 * h:8 * h + 8]], axis=0)
                fg_st[half + 2 * h, a // 2, :, :] = pair.astype(jnp.bfloat16)
        far = half * (high % 2) + (1 - half) * (1 - high % 2)
        copy_to(
            fg_st.at[far * far_cube + (1 - far) * first_cube], fg_in.at[far],
            send_sem.at[9 + far], recv_sem.at[9 + far], 2 * first_cube + core, reflected,
        ).start()

    loop(0, 2, filter_half)

    loop(BACK_A, BACK_B, send_back)
    wait_bytes(fg_in.at[1], recv_sem.at[10])

    def add_half(p):
        part = pl.ds(8 * p, 8)
        terms = fg_st[second_cube, part].astype(jnp.float32) + fg_in[1, part].astype(jnp.float32)
        fg_mid[part] = terms.astype(jnp.bfloat16)

    loop(0, 4, add_half)
    copy_to(
        fg_mid, fg_last, send_sem.at[6], recv_sem.at[6], 2 * second_cube + core, reflected
    ).start()
    loop(BACK_B, 64, send_back)
    wait_bytes(fg_last, recv_sem.at[6])
    wait_bytes(fg_in.at[0], recv_sem.at[9])

    def add_last(p):
        part = pl.ds(8 * p, 8)
        terms = fg_st[high, part].astype(jnp.float32) + fg_in[0, part].astype(jnp.float32)
        terms = terms + fg_last[part].astype(jnp.float32)
        total[pl.ds(16 * p, 16)] = terms.reshape(16, 8, 128)

    loop(0, 4, add_last)
    spread_total()
    wait_bytes(ig_in, recv_sem.at[4])

    def turn_back(i):
        g, j = i // 2, i % 2
        owners = pl.ds(pl.multiple_of(16 * g, 16), 16)
        block = ig_in[owners, j].astype(jnp.float32)
        for at, q in enumerate(QUARTERS):
            cols = pl.ds(pl.multiple_of(512 * (2 * q + j) + 128 * g, 128), 128)
            part = block[:, 8 * at : 8 * at + 8, :].reshape(128, 128)
            ig_out[:, cols] = part.T.astype(jnp.bfloat16)

    loop(0, 8, turn_back)
    wait_bytes(fg_parts, recv_sem.at[5])
    for g in range(4):
        part = fg_parts[pl.ds(16 * g, 16)].reshape(128, 128)
        fg_out[:, pl.ds(128 * g, 128)] = part.T
    for which in (7, 8):
        wait_bytes(sig_in.at[pl.ds(0, 63), pl.ds(0, 32)], send_sem.at[which])
        wait_bytes(sig_in.at[0, pl.ds(0, 16)], send_sem.at[which])
    for which in (0, 4):
        wait_bytes(ig_in.at[pl.ds(0, 63)], send_sem.at[which])
        wait_bytes(ig_in.at[0, 0], send_sem.at[which])
    wait_bytes(filt_in.at[pl.ds(0, 63)], send_sem.at[2])
    wait_bytes(fg_in.at[0], send_sem.at[9])
    wait_bytes(fg_in.at[1], send_sem.at[10])
    wait_bytes(fg_mid, send_sem.at[6])
    wait_bytes(fg_parts.at[pl.ds(0, 63)], send_sem.at[5])


def shards(inputs, grad_out, filt):
    vmem = pl.BlockSpec(memory_space=pltpu.VMEM)
    hbm = pl.BlockSpec(memory_space=pl.ANY)
    tables = [jnp.asarray(t) for t in big_tables()]
    bf16, f32 = jnp.bfloat16, jnp.float32
    input_grad, filter_grad = pl.pallas_call(
        fused_kernel,
        out_shape=(
            jax.ShapeDtypeStruct((128, 4096), bf16),
            jax.ShapeDtypeStruct((128, 512), f32),
        ),
        in_specs=[hbm] * 5,
        out_specs=(vmem, vmem),
        scratch_shapes=[
            pltpu.VMEM((2, 256, 256), bf16),
            pltpu.VMEM((2, 72, 128), f32),
            pltpu.VMEM((128, 4096), bf16),
            pltpu.VMEM((128, 4096), bf16),
            pltpu.VMEM((128, 4096), bf16),
            pltpu.VMEM((64, 2, 32, 128), bf16),
            pltpu.VMEM((64, 2, 32, 128), bf16),
            pltpu.VMEM((64, 32, 128), bf16),
            pltpu.VMEM((64, 64, 128), bf16),
            pltpu.VMEM((64, 64, 128), bf16),
            pltpu.VMEM((64, 32, 128), bf16),
            pltpu.VMEM((KN, 160, 256), bf16),
            pltpu.VMEM((KN, 64, 256), f32),
            pltpu.VMEM((KN, 96, 256), f32),
            pltpu.VMEM((64, 2, 32, 128), bf16),
            pltpu.VMEM((4, 32, 16, 128), bf16),
            pltpu.VMEM((64, 2, 32, 128), bf16),
            pltpu.VMEM((2, 32, 16, 128), bf16),
            pltpu.VMEM((32, 16, 128), bf16),
            pltpu.VMEM((32, 16, 128), bf16),
            pltpu.VMEM((64, 8, 128), f32),
            pltpu.VMEM((64, 8, 128), f32),
            pltpu.SemaphoreType.DMA((5,)),
            pltpu.SemaphoreType.DMA((11,)),
            pltpu.SemaphoreType.DMA((11,)),
        ],
        compiler_params=pltpu.CompilerParams(
            collective_id=0, has_side_effects=True, vmem_limit_bytes=60 * 1024 * 1024
        ),
    )(grad_out[0], inputs[0], filt, *tables)
    return input_grad[None], filter_grad


def solution(mesh):
    in_specs = (P("dp", "ctx", None), P("dp", "ctx", None), P("ctx", None))
    out_specs = (P("dp", "ctx", None), P("ctx", "dp"))
    return jax.shard_map(shards, mesh=mesh, in_specs=in_specs, out_specs=out_specs, check_vma=False)
```

```python
import math
import numpy as np
import jax
import jax.numpy as jnp
from jax import lax
from jax.experimental import pallas as pl
from jax.experimental.pallas import tpu as pltpu
from jax.sharding import PartitionSpec as P

N = 16384
KN = 65
KC = 13
BACK_A, BACK_B = 32, 52
QUARTERS = (0, 2, 1, 3)


def cmul_const(v, c, s):
    re, im = v
    if abs(s) < 1e-12 and abs(c - 1) < 1e-12:
        return v
    if abs(c) < 1e-12 and abs(s - 1) < 1e-12:
        return (-im, re)
    if abs(c) < 1e-12 and abs(s + 1) < 1e-12:
        return (im, -re)
    if abs(abs(c) - abs(s)) < 1e-12:
        h = abs(c)
        sc, ss = (1.0 if c > 0 else -1.0), (1.0 if s > 0 else -1.0)
        a = re * h
        b = im * h
        first = (a if sc > 0 else -a)
        first = first - b if ss > 0 else first + b
        second = (b if sc > 0 else -b)
        second = second + a if ss > 0 else second - a
        return (first, second)
    return (re * c - im * s, re * s + im * c)


def fft_complex(values, sign):
    n = len(values)
    if n == 1:
        return values
    if n == 2:
        (ar, ai), (br, bi) = values
        return [(ar + br, ai + bi), (ar - br, ai - bi)]
    if n % 4 == 0:
        quarter = n // 4
        parts = [fft_complex(values[r::4], sign) for r in range(4)]
        out = [None] * n
        for k in range(quarter):
            turned = []
            for r in range(4):
                angle = sign * 2.0 * math.pi * r * k / n
                turned.append(cmul_const(parts[r][k], math.cos(angle), math.sin(angle)))
            (ar, ai), (br, bi), (cr, ci), (dr, di) = turned
            s0r, s0i, s1r, s1i = ar + cr, ai + ci, ar - cr, ai - ci
            s2r, s2i, s3r, s3i = br + dr, bi + di, br - dr, bi - di
            out[k] = (s0r + s2r, s0i + s2i)
            out[k + 2 * quarter] = (s0r - s2r, s0i - s2i)
            if sign < 0:
                out[k + quarter] = (s1r + s3i, s1i - s3r)
                out[k + 3 * quarter] = (s1r - s3i, s1i + s3r)
            else:
                out[k + quarter] = (s1r - s3i, s1i + s3r)
                out[k + 3 * quarter] = (s1r + s3i, s1i - s3r)
        return out
    half = n // 2
    even = fft_complex(values[0::2], sign)
    odd = fft_complex(values[1::2], sign)
    out = [None] * n
    for k in range(half):
        angle = sign * 2.0 * math.pi * k / n
        tr, ti = cmul_const(odd[k], math.cos(angle), math.sin(angle))
        er, ei = even[k]
        out[k] = (er + tr, ei + ti)
        out[k + half] = (er - tr, ei - ti)
    return out


def odd_bins(values, period):
    quarter = period // 4
    turned = []
    for a in range(quarter):
        angle = -2.0 * math.pi * a / period
        turned.append(cmul_const((values[a], -values[a + quarter]), math.cos(angle), math.sin(angle)))
    spectrum = fft_complex(turned, -1.0)
    found = {}
    for l in range(quarter):
        k = 4 * l + 1
        re, im = spectrum[l]
        if k <= period // 2:
            found[k] = (re, im)
        else:
            found[period - k] = (re, -im)
    return found


def real_bins(values):
    n = len(values)
    if n == 2:
        return {0: (values[0] + values[1], None), 1: (values[0] - values[1], None)}
    half = n // 2
    sums = [values[a] + values[a + half] for a in range(half)]
    diffs = [values[a] - values[a + half] for a in range(half)]
    found = {2 * k: v for k, v in real_bins(sums).items()}
    found.update(odd_bins(diffs, n))
    return found


def padded_bins(values):
    found = odd_bins(values, 2 * len(values))
    found.update({2 * k: v for k, v in real_bins(values).items()})
    return found


def odd_values(bins, period):
    quarter = period // 4
    spectrum = []
    for l in range(quarter):
        k = 4 * l + 1
        if k <= period // 2:
            spectrum.append(bins[k])
        else:
            re, im = bins[period - k]
            spectrum.append((re, -im))
    turned = fft_complex(spectrum, 1.0)
    lower, upper = [], []
    for a in range(quarter):
        angle = 2.0 * math.pi * a / period
        re, im = cmul_const(turned[a], math.cos(angle), math.sin(angle))
        lower.append(re)
        upper.append(-im)
    return lower + upper


def real_values(bins, n):
    if n == 2:
        return [bins[0][0] + bins[1][0], bins[0][0] - bins[1][0]]
    sums = real_values({k // 2: v for k, v in bins.items() if k % 2 == 0}, n // 2)
    diffs = odd_values(bins, n)
    return [s + d for s, d in zip(sums, diffs)] + [s - d for s, d in zip(sums, diffs)]


def padded_values(bins, n):
    odd = odd_values(bins, 2 * n)
    even = real_values({k // 2: v for k, v in bins.items() if k % 2 == 0}, n)
    return [o + e for o, e in zip(odd, even)]


def big_tables():
    m = np.arange(128)
    grid = (m[:, None] * m[None, :] % 128) * (2.0 * np.pi / 128)
    c, s = np.cos(grid), np.sin(grid)
    full = np.block([[c, -s], [s, c]]).astype(np.float32)
    high = full.astype(jnp.bfloat16)
    low = (full - high.astype(np.float32)).astype(jnp.bfloat16)
    turn = np.arange(72)[:, None] * m[None, :] * (2.0 * np.pi / N)
    return np.stack([high, low]), np.stack([np.cos(turn), np.sin(turn)]).astype(np.float32)


def spectra_of(src_ref, y_ref, tw_ref, group, place):
    rows = pl.ds(pl.multiple_of(group * 16, 16), 16)
    kept = pl.ds(pl.multiple_of(place * 16, 16), 16)
    bins = padded_bins([src_ref[a, rows, :].astype(jnp.float32) for a in range(64)])
    for k in range(KN):
        re, im = bins[k]
        tr, ti = tw_ref[0, pl.ds(k, 1), :], tw_ref[1, pl.ds(k, 1), :]
        if im is None:
            re, im = re * tr, -(re * ti)
        else:
            re, im = re * tr + im * ti, im * tr - re * ti
        y_ref[k, kept, pl.ds(0, 128)] = re.astype(jnp.bfloat16)
        y_ref[k, kept, pl.ds(128, 128)] = im.astype(jnp.bfloat16)


def forward_dot(y_ref, k0, first, rows, tab_ref):
    y = y_ref[pl.ds(k0, KC), pl.ds(first, rows), :].reshape(KC * rows, 256)
    spec = jnp.dot(y, tab_ref[0], preferred_element_type=jnp.float32)
    spec = spec + jnp.dot(y, tab_ref[1], preferred_element_type=jnp.float32)
    return spec.reshape(KC, rows, 256)


def inverse_dot(prods, tab_ref):
    prod = jnp.concatenate(prods, axis=0)
    form = (((1,), (1,)), ((), ()))
    back = lax.dot_general(prod, tab_ref[0], form, preferred_element_type=jnp.float32)
    back = back + lax.dot_general(prod, tab_ref[1], form, preferred_element_type=jnp.float32)
    return back.reshape(KC, prod.shape[0] // KC, 256)


def conj_product(x, u):
    xr, xi = x[:, :128], x[:, 128:]
    ur, ui = u[:, :128], u[:, 128:]
    return xr * ur + xi * ui, xr * ui - xi * ur


def values_of(v_ref, tw_ref, rows):
    bins = {}
    for k in range(KN):
        re, im = v_ref[k, rows, pl.ds(0, 128)], v_ref[k, rows, pl.ds(128, 128)]
        tr, ti = tw_ref[0, pl.ds(k, 1), :], tw_ref[1, pl.ds(k, 1), :]
        if k in (0, 64):
            bins[k] = (re * tr - im * ti, None)
        else:
            bins[k] = (re * tr - im * ti, im * tr + re * ti)
    return padded_values(bins, 64)


def copy_to(src, dst, send_sem, recv_sem, dp, ctx):
    return pltpu.make_async_remote_copy(
        src_ref=src,
        dst_ref=dst,
        send_sem=send_sem,
        recv_sem=recv_sem,
        device_id=(dp, ctx),
        device_id_type=pl.DeviceIdType.MESH,
    )


def wait_bytes(ref, sem):
    pltpu.make_async_copy(ref, ref, sem).wait()


def partner(me, i):
    return ((me // 16 + i % 4) % 4) * 16 + (me % 16 + i // 4) % 16


def to_pieces(x_ref, st_ref, g, j, index):
    parts = []
    for q in QUARTERS:
        cols = pl.ds(pl.multiple_of(512 * (2 * q + j) + 128 * g, 128), 128)
        parts.append(x_ref[:, cols].astype(jnp.float32).T.reshape(16, 8, 128))
    owners = pl.ds(pl.multiple_of(16 * g, 16), 16)
    index(owners)[...] = jnp.concatenate(parts, axis=1).astype(jnp.bfloat16)


def loop(start, stop, step):
    def run(i, carry):
        step(i)
        return carry

    lax.fori_loop(start, stop, run, 0)


def fused_kernel(
    up_hbm, sig_hbm, filt_hbm, tab_hbm, tw_hbm,
    ig_out, fg_out,
    tab_ref, tw_ref,
    up_x, sig_x, filt_x, up_st, sig_st, filt_st, up_in, sig_in, filt_in,
    y_ref, u_ref, v_ref, ig_st, fg_st, ig_in, fg_in, fg_mid, fg_last, total, fg_parts,
    load_sem, send_sem, recv_sem,
):
    dp = lax.axis_index("dp")
    me = lax.axis_index("ctx")
    core, high = dp % 2, dp // 2
    plane, place = me // 16, me % 16
    mesh_id = pl.DeviceIdType.MESH

    def owner(cube, c):
        odd = cube % 2
        z = c // 16
        return 16 * (odd * z + (1 - odd) * (3 - z)) + c % 16

    mine = owner(high, me)
    late = mine // 32
    flip, mirror = high + 1 - 2 * (high % 2), 3 - high
    first_cube = (1 - late) * flip + late * mirror
    second_cube = (1 - late) * mirror + late * flip
    far_cube = 3 - flip
    reflected = (3 - plane) * 16 + place

    loads = [
        pltpu.make_async_copy(src, dst, load_sem.at[i])
        for i, (src, dst) in enumerate(
            (
                (up_hbm, up_x), (filt_hbm, filt_x), (sig_hbm, sig_x),
                (tab_hbm, tab_ref), (tw_hbm, tw_ref),
            )
        )
    ]
    for load in loads:
        load.start()
    barrier = pltpu.get_barrier_semaphore()

    def hail(there, c):
        pl.semaphore_signal(barrier, inc=1, device_id=(there, c), device_id_type=mesh_id)

    hail(2 * high + 1 - core, me)
    hail(2 * first_cube + core, reflected)
    hail(2 * second_cube + core, reflected)

    def greet(i):
        c = partner(me, i)
        for j in range(2):
            hail(2 * high + j, c)

    loop(1, 64, greet)

    def greet_outside(i):
        step = i // 16
        lower = 1 - plane // 2
        z = lower * (-1 - step) + (1 - lower) * (4 + step)
        there = (high + z // 4 + 4) % 4
        hail(2 * there + core, (z % 4) * 16 + (place + i) % 16)

    outer = 1 - (plane % 3 + 1) // 2
    loop(0, 16 * (1 + outer), greet_outside)

    def turn_signal(x_ref, st_ref):
        def turn(i):
            g, j = i // 2, i % 2
            to_pieces(x_ref, st_ref, g, j, lambda owners: st_ref.at[owners, j])

        loop(0, 8, turn)

    def spread(src_ref, piece, dst_ref, slot, which):
        def begin():
            here = piece(me)
            pltpu.make_async_copy(
                src_ref.at[here, core], dst_ref.at[slot], recv_sem.at[which]
            ).start()
            copy_to(
                src_ref.at[here, 1 - core], dst_ref.at[slot], send_sem.at[which],
                recv_sem.at[which], 2 * high + 1 - core, me,
            ).start()

        def send(i):
            c = partner(me, i)
            for j in range(2):
                copy_to(
                    src_ref.at[piece(c), j], dst_ref.at[slot], send_sem.at[which],
                    recv_sem.at[which], 2 * high + j, c,
                ).start()

        return begin, send

    def spread_all(*args):
        begin, send = spread(*args)
        begin()
        loop(1, 64, send)

    def send_signal_half(half):
        part = pl.ds(16 * half, 16)
        slot = (me, pl.ds(pl.multiple_of(32 * core + 16 * half, 16), 16))
        sems = send_sem.at[7 + half], recv_sem.at[7 + half]
        pltpu.make_async_copy(sig_st.at[mine, core, part], sig_in.at[slot], sems[1]).start()
        copy_to(
            sig_st.at[mine, 1 - core, part], sig_in.at[slot], *sems, 2 * high + 1 - core, me
        ).start()

        def send(i):
            c = partner(me, i)
            for j in range(2):
                copy_to(
                    sig_st.at[owner(high, c), j, part], sig_in.at[slot], *sems, 2 * high + j, c
                ).start()

        loop(1, 64, send)

    def spread_filter():
        pltpu.make_async_copy(filt_st.at[mine], filt_in.at[me], recv_sem.at[2]).start()

        def send(i):
            there = (place + i // 4) % 16
            even = 1 - (there // 4 + there % 4) % 2
            ahead = i % 4
            step = ahead - 4 * (ahead // 3) - 4 * (1 - even) * (1 - ahead % 2) * (ahead // 2)
            z = (4 * high + plane + step + 16) % 16
            cube = z // 4
            c = (z % 4) * 16 + there
            copy_to(
                filt_st.at[owner(cube, c)], filt_in.at[me], send_sem.at[2], recv_sem.at[2],
                2 * cube + core, c,
            ).start()

        loop(1, 64, send)

    def spread_total():
        pltpu.make_async_copy(total.at[me], fg_parts.at[mine], recv_sem.at[5]).start()

        def send(i):
            c = partner(me, i)
            copy_to(
                total.at[c], fg_parts.at[mine], send_sem.at[5], recv_sem.at[5], dp, c
            ).start()

        loop(1, 64, send)

    loads[0].wait()
    turn_signal(up_x, up_st)
    pl.semaphore_wait(barrier, 129 + 16 * (1 + outer))
    rows = pl.ds(pl.multiple_of(32 * core, 32), 32)
    spread_all(up_st, lambda c: owner(high, c), up_in, (me, rows), 0)
    loads[1].wait()
    loop(0, 4, lambda g: to_pieces(filt_x, filt_st, g, core, lambda owners: filt_st.at[owners]))
    spread_filter()
    loads[2].wait()
    turn_signal(sig_x, sig_st)
    for half in range(2):
        send_signal_half(half)
    loads[3].wait()
    loads[4].wait()

    wait_bytes(up_in, recv_sem.at[0])
    loop(0, 4, lambda g: spectra_of(up_in, y_ref, tw_ref, g, g))

    def up_spectra(step):
        k0 = step * KC
        spec = forward_dot(y_ref, k0, 0, 64, tab_ref)
        for i in range(KC):
            k = k0 + i
            scale = jnp.where((k == 0) | (k == 64), 1.0 / N, 2.0 / N).astype(jnp.float32)
            u_ref[k] = spec[i] * scale

    loop(0, KN // KC, up_spectra)

    wait_bytes(filt_in, recv_sem.at[2])
    loop(0, 2, lambda g: spectra_of(filt_in, y_ref, tw_ref, g, 8 + g))

    def input_products(step):
        k0 = step * KC
        spec = forward_dot(y_ref, k0, 128, 32, tab_ref)
        prods = []
        for i in range(KC):
            both = jnp.concatenate([spec[i], spec[i]], axis=0)
            re, im = conj_product(both, u_ref[k0 + i])
            prods.append(jnp.concatenate([re, im], axis=1).astype(jnp.bfloat16))
        v_ref[pl.ds(k0, KC), pl.ds(0, 64), :] = inverse_dot(prods, tab_ref)

    loop(0, KN // KC, input_products)

    def input_values(group):
        rows = pl.ds(pl.multiple_of(group * 16, 16), 16)
        out = values_of(v_ref, tw_ref, rows)
        kept = pl.ds(pl.multiple_of((group % 2) * 16, 16), 16)
        for a in range(64):
            ig_st[a, group // 2, kept, :] = out[a].astype(jnp.bfloat16)

    loop(0, 4, input_values)
    begin_back, send_back = spread(ig_st, lambda c: c, ig_in, (mine, core), 4)
    begin_back()
    loop(1, BACK_A, send_back)

    def filter_half(half):
        wait_bytes(sig_in.at[:, pl.ds(0, 32)], recv_sem.at[7 + half])
        loop(0, 2, lambda g: spectra_of(sig_in, y_ref, tw_ref, 2 * g + half, 4 + 2 * half + g))
        first_row = pl.multiple_of(64 + 32 * half, 32)
        above = pl.ds(pl.multiple_of(16 * half, 16), 16)
        below = pl.ds(pl.multiple_of(32 + 16 * half, 16), 16)
        rows = pl.ds(pl.multiple_of(64 + 16 * half, 16), 16)

        def filter_products(step):
            k0 = step * KC
            spec = forward_dot(y_ref, k0, first_row, 32, tab_ref)
            prods = []
            for i in range(KC):
                u = jnp.concatenate([u_ref[k0 + i, above, :], u_ref[k0 + i, below, :]], axis=0)
                re, im = conj_product(spec[i], u)
                re, im = re[0:16] + re[16:32], im[0:16] + im[16:32]
                prods.append(jnp.concatenate([re, im], axis=1).astype(jnp.bfloat16))
            v_ref[pl.ds(k0, KC), rows, :] = inverse_dot(prods, tab_ref)

        loop(0, KN // KC, filter_products)
        out = values_of(v_ref, tw_ref, rows)
        for a in range(0, 64, 2):
            for h in range(2):
                pair = jnp.concatenate([out[a][8 * h:8 * h + 8], out[a + 1][8 * h:8 * h + 8]], axis=0)
                fg_st[half + 2 * h, a // 2, :, :] = pair.astype(jnp.bfloat16)
        far = half * (high % 2) + (1 - half) * (1 - high % 2)
        copy_to(
            fg_st.at[far * far_cube + (1 - far) * first_cube], fg_in.at[far],
            send_sem.at[9 + far], recv_sem.at[9 + far], 2 * first_cube + core, reflected,
        ).start()

    loop(0, 2, filter_half)

    loop(BACK_A, BACK_B, send_back)
    wait_bytes(fg_in.at[1], recv_sem.at[10])

    def add_half(p):
        part = pl.ds(8 * p, 8)
        terms = fg_st[second_cube, part].astype(jnp.float32) + fg_in[1, part].astype(jnp.float32)
        fg_mid[part] = terms.astype(jnp.bfloat16)

    loop(0, 4, add_half)
    copy_to(
        fg_mid, fg_last, send_sem.at[6], recv_sem.at[6], 2 * second_cube + core, reflected
    ).start()
    wait_bytes(fg_last, recv_sem.at[6])
    wait_bytes(fg_in.at[0], recv_sem.at[9])

    def add_last(p):
        part = pl.ds(8 * p, 8)
        terms = fg_st[high, part].astype(jnp.float32) + fg_in[0, part].astype(jnp.float32)
        terms = terms + fg_last[part].astype(jnp.float32)
        total[pl.ds(16 * p, 16)] = terms.reshape(16, 8, 128)

    loop(0, 4, add_last)
    spread_total()
    loop(BACK_B, 64, send_back)
    wait_bytes(ig_in, recv_sem.at[4])

    def turn_back(i):
        g, j = i // 2, i % 2
        owners = pl.ds(pl.multiple_of(16 * g, 16), 16)
        block = ig_in[owners, j].astype(jnp.float32)
        for at, q in enumerate(QUARTERS):
            cols = pl.ds(pl.multiple_of(512 * (2 * q + j) + 128 * g, 128), 128)
            part = block[:, 8 * at : 8 * at + 8, :].reshape(128, 128)
            ig_out[:, cols] = part.T.astype(jnp.bfloat16)

    loop(0, 8, turn_back)
    wait_bytes(fg_parts, recv_sem.at[5])
    for g in range(4):
        part = fg_parts[pl.ds(16 * g, 16)].reshape(128, 128)
        fg_out[:, pl.ds(128 * g, 128)] = part.T
    for which in (7, 8):
        wait_bytes(sig_in.at[pl.ds(0, 63), pl.ds(0, 32)], send_sem.at[which])
        wait_bytes(sig_in.at[0, pl.ds(0, 16)], send_sem.at[which])
    for which in (0, 4):
        wait_bytes(ig_in.at[pl.ds(0, 63)], send_sem.at[which])
        wait_bytes(ig_in.at[0, 0], send_sem.at[which])
    wait_bytes(filt_in.at[pl.ds(0, 63)], send_sem.at[2])
    wait_bytes(fg_in.at[0], send_sem.at[9])
    wait_bytes(fg_in.at[1], send_sem.at[10])
    wait_bytes(fg_mid, send_sem.at[6])
    wait_bytes(fg_parts.at[pl.ds(0, 63)], send_sem.at[5])


def shards(inputs, grad_out, filt):
    vmem = pl.BlockSpec(memory_space=pltpu.VMEM)
    hbm = pl.BlockSpec(memory_space=pl.ANY)
    tables = [jnp.asarray(t) for t in big_tables()]
    bf16, f32 = jnp.bfloat16, jnp.float32
    input_grad, filter_grad = pl.pallas_call(
        fused_kernel,
        out_shape=(
            jax.ShapeDtypeStruct((128, 4096), bf16),
            jax.ShapeDtypeStruct((128, 512), f32),
        ),
        in_specs=[hbm] * 5,
        out_specs=(vmem, vmem),
        scratch_shapes=[
            pltpu.VMEM((2, 256, 256), bf16),
            pltpu.VMEM((2, 72, 128), f32),
            pltpu.VMEM((128, 4096), bf16),
            pltpu.VMEM((128, 4096), bf16),
            pltpu.VMEM((128, 4096), bf16),
            pltpu.VMEM((64, 2, 32, 128), bf16),
            pltpu.VMEM((64, 2, 32, 128), bf16),
            pltpu.VMEM((64, 32, 128), bf16),
            pltpu.VMEM((64, 64, 128), bf16),
            pltpu.VMEM((64, 64, 128), bf16),
            pltpu.VMEM((64, 32, 128), bf16),
            pltpu.VMEM((KN, 160, 256), bf16),
            pltpu.VMEM((KN, 64, 256), f32),
            pltpu.VMEM((KN, 96, 256), f32),
            pltpu.VMEM((64, 2, 32, 128), bf16),
            pltpu.VMEM((4, 32, 16, 128), bf16),
            pltpu.VMEM((64, 2, 32, 128), bf16),
            pltpu.VMEM((2, 32, 16, 128), bf16),
            pltpu.VMEM((32, 16, 128), bf16),
            pltpu.VMEM((32, 16, 128), bf16),
            pltpu.VMEM((64, 8, 128), f32),
            pltpu.VMEM((64, 8, 128), f32),
            pltpu.SemaphoreType.DMA((5,)),
            pltpu.SemaphoreType.DMA((11,)),
            pltpu.SemaphoreType.DMA((11,)),
        ],
        compiler_params=pltpu.CompilerParams(
            collective_id=0, has_side_effects=True, vmem_limit_bytes=60 * 1024 * 1024
        ),
    )(grad_out[0], inputs[0], filt, *tables)
    return input_grad[None], filter_grad


def solution(mesh):
    in_specs = (P("dp", "ctx", None), P("dp", "ctx", None), P("ctx", None))
    out_specs = (P("dp", "ctx", None), P("ctx", "dp"))
    return jax.shard_map(shards, mesh=mesh, in_specs=in_specs, out_specs=out_specs, check_vma=False)
```
